256 devices in a mesh: dp: 16 (over x, y_hi, core), etp: 16 (over z, y_lo).
Axes of the slice: x: 4, y: 4 (y_hi: 2, y_lo: 2; y = y_hi * 2 + y_lo), z: 8, core: 2. Of those that a mesh axis runs over, the one named last changes fastest.
Arguments:
- tokens: bfloat16 [32768, 3072], P(('dp', 'etp')), may hold values from -24 to 24
- out_grad: bfloat16 [32768, 3072], P(('dp', 'etp')), may hold values from -4 to 4
- route_ids: int32 [32768, 2], P(('dp', 'etp')), may hold values from 0 to 7, as said below
- route_prob: bfloat16 [32768], P(('dp', 'etp')), may hold values from 0.19921875 to 1
- w_gate: bfloat16 [3072, 8192], P(None, 'etp'), may hold values from -0.109375 to 0.109375
- w_up: bfloat16 [3072, 8192], P(None, 'etp'), may hold values from -0.109375 to 0.109375
- w_down: bfloat16 [8192, 3072], P('etp'), may hold values from -0.0625 to 0.0625
Outputs:
- grad_tokens: bfloat16 [32768, 3072], P(('dp', 'etp'))
- grad_prob: float32 [32768], P(('dp', 'etp'))
- grad_gate: bfloat16 [3072, 8192], P('dp', 'etp')
- grad_up: bfloat16 [3072, 8192], P('dp', 'etp')
- grad_down: bfloat16 [8192, 3072], P('etp', 'dp')
The draws below stay inside these ranges and needn't reach their ends.
Inputs may be any that keep to these rules, and one draw needn't show every extreme that they name: `route_ids`: each row names two different experts. In each aligned block of 128 rows (the rows of one device) between 24 and 32 rows name expert 0, and in some block exactly 32 rows do.
All inputs are finite; a program needn't handle non-finite values.
Results may differ from the reference program's by a relative error of at most 0.023.
Values may be sent and summed in bfloat16 or wider, within the bound.
A program may use at most 128 MiB of HBM per device.

```python
import jax
import jax.numpy as jnp
from jax import lax

D = 3072
FF = 8192
EXPERTS = 8
TOK_DEV = 128
LOC_CAP = 32
TOKENS = 32768
N_DP = 16
N_ETP = 16


def draw_route_ids(key, part):
    key = jax.random.fold_in(key, 11)
    subkeys = jax.random.split(key, 6)
    blocks = TOKENS // TOK_DEV
    counts = jax.random.randint(subkeys[0], (blocks,), LOC_CAP * 3 // 4, LOC_CAP + 1)
    fullest = jax.random.randint(subkeys[1], (), 0, blocks)
    counts = jnp.where(jnp.arange(blocks) == fullest, LOC_CAP, counts)
    ranking = jax.vmap(lambda sub_key: jax.random.permutation(sub_key, TOK_DEV))(jax.random.split(subkeys[2], blocks))
    chosen = ranking < counts[:, None]
    primary = jax.random.randint(subkeys[3], (blocks, TOK_DEV), 1, EXPERTS)
    step_off = jax.random.randint(subkeys[4], (blocks, TOK_DEV), 1, EXPERTS - 1)
    secondary = 1 + (primary - 1 + step_off) % (EXPERTS - 1)
    placing = jax.random.randint(subkeys[5], (blocks, TOK_DEV), 0, 2)
    slot_a = jnp.where(chosen, jnp.where(placing == 0, 0, primary), primary)
    slot_b = jnp.where(chosen, jnp.where(placing == 0, primary, 0), secondary)
    return jnp.stack([slot_a, slot_b], axis=-1).reshape(TOKENS, 2).astype(jnp.int32)


def spiked(array, stream_key, source, target, blocks, factor):
    owner, partner = [(jnp.arange(array.shape[position]) // (array.shape[position] // blocks)).reshape([-1 if axis == position else 1 for axis in range(array.ndim)]) for position in (source, target)]
    chosen = jax.random.permutation(stream_key, blocks)[partner]
    strong = (owner == chosen) | (owner == (partner + blocks // 2) % blocks)
    return jnp.where(strong, factor * array, array)


def level_of(own_key, extent, pieces, least, high):
    level, own = 1.0, jax.random.fold_in(own_key, 6)
    for axis_at, blocks in pieces:
        heights = jnp.exp(jax.random.uniform(jax.random.fold_in(own, axis_at), (blocks,), jnp.float32, least / len(pieces), high / len(pieces)))
        level = level * jnp.repeat(heights, extent[axis_at] // blocks).reshape([-1 if axis == axis_at else 1 for axis in range(len(extent))])
    return level


def normal_values(key, extent, width, reach, pieces=(), kind=jnp.bfloat16):
    array = width * jax.random.normal(key, extent, jnp.float32)
    if pieces:
        array = array * level_of(key, extent, pieces, -0.22, 0.18)
    return jnp.clip(array, -reach, reach).astype(kind)


def heavy_noise(key, dims, deviation, limit, shards, heavy, kind=jnp.bfloat16):
    array = deviation * jax.random.normal(key, dims, jnp.float32)
    if shards:
        array = array * level_of(key, dims, shards, -0.22, 0.18)
    return jnp.clip(spiked(array, jax.random.fold_in(key, 3), *heavy), -limit, limit).astype(kind)


def setup_inputs(seed: int = 0) -> dict:
    key_of = jax.random.split(jax.random.key(seed), 8)
    tokens = heavy_noise(key_of[0], (TOKENS, D), 1.0, 24.0, ((0, 256),), (0, 1, 256, 6.0))
    out_grad = normal_values(key_of[1], (TOKENS, D), 0.5, 4.0, ((0, 256),))
    route_ids = draw_route_ids(jax.random.fold_in(key_of[7], 71), 0)
    route_prob = jnp.clip(0.19921875 + 0.80078125 * jax.random.uniform(key_of[3], (TOKENS,), jnp.float32) ** level_of(key_of[3], (TOKENS,), ((0, 256),), -0.2, 0.2), 0.19921875, 1.0).astype(jnp.bfloat16)
    w_gate = normal_values(key_of[4], (D, FF), D ** -0.5, 0.109375, ((1, 16),))
    w_up = normal_values(key_of[5], (D, FF), D ** -0.5, 0.109375, ((1, 16),))
    w_down = normal_values(key_of[6], (FF, D), FF ** -0.5, 0.0625, ((0, 16),))
    return {"tokens": tokens, "out_grad": out_grad, "route_ids": route_ids, "route_prob": route_prob, "w_gate": w_gate, "w_up": w_up, "w_down": w_down}


def reference(tokens, out_grad, route_ids, route_prob, w_gate, w_up, w_down):
    total = tokens.shape[0]
    model_width = tokens.shape[1]
    block_width = FF // N_ETP
    slots = N_DP * N_ETP * LOC_CAP
    routed = jnp.logical_or(route_ids[:, 0] == 0, route_ids[:, 1] == 0)
    positions = jnp.arange(total, dtype=jnp.int32)
    packed_order = jnp.argsort(jnp.where(routed, positions, positions + total))[:slots].astype(jnp.int32)
    x_rows = tokens[packed_order]
    dy_rows = out_grad[packed_order]
    row_weight = jnp.where(routed, route_prob, jnp.zeros_like(route_prob))[packed_order]
    row_scale = row_weight.astype(jnp.float32)[:, None]
    gate_blocks = w_gate.reshape(model_width, N_ETP, block_width).transpose(1, 0, 2)
    up_blocks = w_up.reshape(model_width, N_ETP, block_width).transpose(1, 0, 2)
    down_blocks = w_down.reshape(N_ETP, block_width, model_width)

    def one_block(carry, blocks):
        token_acc, prob_acc = carry
        gate_w, up_w, down_w = blocks
        gate_pre = jnp.dot(x_rows, gate_w, preferred_element_type=jnp.float32)
        up_pre = jnp.dot(x_rows, up_w, preferred_element_type=jnp.float32)
        sig_gate = jax.nn.sigmoid(gate_pre)
        act_gate = gate_pre * sig_gate
        hidden = (act_gate * up_pre).astype(jnp.bfloat16)
        scaled = (row_scale * hidden.astype(jnp.float32)).astype(jnp.bfloat16)
        hidden_raw = jnp.dot(dy_rows, down_w.T, preferred_element_type=jnp.float32)
        prob_acc = prob_acc + jnp.sum(hidden.astype(jnp.float32) * hidden_raw, axis=1)
        grad_hidden = row_scale * hidden_raw
        grad_gate_pre = (grad_hidden * up_pre * sig_gate * (1.0 + gate_pre * (1.0 - sig_gate))).astype(jnp.bfloat16)
        grad_up_pre = (grad_hidden * act_gate).astype(jnp.bfloat16)
        token_part = jnp.dot(grad_gate_pre, gate_w.T, preferred_element_type=jnp.float32)
        token_part = token_part + jnp.dot(grad_up_pre, up_w.T, preferred_element_type=jnp.float32)
        token_part = lax.optimization_barrier(token_part.astype(jnp.bfloat16)).astype(jnp.float32)
        gate_grad = jnp.dot(x_rows.T, grad_gate_pre, preferred_element_type=jnp.float32)
        up_grad = jnp.dot(x_rows.T, grad_up_pre, preferred_element_type=jnp.float32)
        down_grad = jnp.dot(scaled.T, dy_rows, preferred_element_type=jnp.float32)
        return (token_acc + token_part, prob_acc), (gate_grad, up_grad, down_grad)

    start_carry = (jnp.zeros((slots, model_width), jnp.float32), jnp.zeros((slots,), jnp.float32))
    (token_acc, prob_acc), (gate_parts, up_parts, down_parts) = lax.scan(
        one_block, start_carry, (gate_blocks, up_blocks, down_blocks))
    grad_gate = (gate_parts.transpose(1, 0, 2).reshape(model_width, FF) / N_DP).astype(jnp.bfloat16)
    grad_up = (up_parts.transpose(1, 0, 2).reshape(model_width, FF) / N_DP).astype(jnp.bfloat16)
    grad_down = (down_parts.reshape(FF, model_width) / N_DP).astype(jnp.bfloat16)
    grad_tokens = jnp.zeros((total, model_width), jnp.bfloat16).at[packed_order].set(token_acc.astype(jnp.bfloat16))
    live_rows = routed[packed_order].astype(jnp.float32)
    grad_prob = jnp.zeros((total,), jnp.float32).at[packed_order].set(prob_acc * live_rows)
    return grad_tokens, grad_prob, grad_gate, grad_up, grad_down
```

```python
import functools

import jax
import jax.numpy as jnp
from jax import lax
from jax.experimental import pallas as pl
from jax.experimental.pallas import tpu as pltpu
from jax.sharding import PartitionSpec as P

MESH = pl.DeviceIdType.MESH
CAP = 32
BF = jnp.bfloat16
F32 = jnp.float32

ORDER = (
    (0, 0), (1, 0), (0, 1), (0, -1),
    (0, 2), (0, -2), (1, 1), (1, -1),
    (0, 3), (0, -3), (0, 4), (1, 2),
    (1, -2), (1, 3), (1, -3), (1, 4),
)
SLOT = {key: i for i, key in enumerate(ORDER)}
CHUNKS = ((2, 1), (2, 0), (1, 1), (-1, 1), (1, 0), (-1, 0), (0, 1), (0, 0))
CIDX = {key: i for i, key in enumerate(CHUNKS)}


def pair_row(col, off):
    return ((off % 8) * 2 + col) * CAP


def dot(a, b):
    return jnp.dot(a, b, preferred_element_type=F32)


def dot_t(a, b):
    return lax.dot_general(a, b, (((1,), (1,)), ((), ())), preferred_element_type=F32)


def kernel(
    ids, prob, tokens, out_grad, w_gate_h, w_up_h, w_down_h,
    o_tok, o_prob, o_w,
    wg, wu, wd, xs, ds, xt, dt, gs, tp, pb, ws, sr, xa, xb, yb, rp, rph, pr, ry, pry,
    w_sem, s_sem, r_sem,
):
    D = tokens.shape[1]
    F = wg.shape[1]
    H = D // 2
    rows_own = o_w.shape[1]
    half = rows_own // 2
    dp, etp = lax.axis_index("dp"), lax.axis_index("etp")
    x, yh, core = dp // 4, (dp // 2) % 2, dp % 2
    z, yl = etp // 2, etp % 2

    def dp_of(px, ph, pc):
        return px * 4 + ph * 2 + pc

    dev = {
        "z+": (dp, ((z + 1) % 8) * 2 + yl),
        "z-": (dp, ((z + 7) % 8) * 2 + yl),
        "yl": (dp, z * 2 + 1 - yl),
        "x+": (dp_of((x + 1) % 4, yh, core), etp),
        "x-": (dp_of((x + 3) % 4, yh, core), etp),
        "y2": (dp_of(x, 1 - yh, core), etp),
        "c": (dp_of(x, yh, 1 - core), etp),
    }

    loads = []
    for i, (src, dst) in enumerate(((w_gate_h, wg), (w_up_h, wu), (w_down_h, wd))):
        cp = pltpu.make_async_copy(src, dst, w_sem.at[i])
        cp.start()
        loads.append(cp)

    barrier = pltpu.get_barrier_semaphore()
    for name in dev:
        pl.semaphore_signal(barrier, inc=1, device_id=dev[name], device_id_type=MESH)

    count = [0]
    sent = []

    def send(name, src, dst):
        i = count[0]
        count[0] += 1
        cp = pltpu.make_async_remote_copy(
            src_ref=src, dst_ref=dst, send_sem=s_sem.at[i], recv_sem=r_sem.at[i],
            device_id=dev[name], device_id_type=MESH,
        )
        cp.start()
        sent.append(cp)
        return cp

    routed = jnp.logical_or(ids[0:1, :] == 0, ids[1:2, :] == 0)
    n_tok = routed.shape[1]
    routed_f = jnp.where(routed, 1.0, 0.0).astype(F32)
    before = (
        lax.broadcasted_iota(jnp.int32, (n_tok, n_tok), 0)
        < lax.broadcasted_iota(jnp.int32, (n_tok, n_tok), 1)
    )
    rank = dot(
        jnp.broadcast_to(routed_f, (16, n_tok)).astype(BF),
        jnp.where(before, 1.0, 0.0).astype(BF),
    )[0:1, :]
    slot_no = lax.broadcasted_iota(jnp.int32, (CAP, n_tok), 0).astype(F32)
    sel = jnp.where(
        jnp.logical_and(
            jnp.broadcast_to(rank, (CAP, n_tok)) == slot_no,
            jnp.broadcast_to(routed_f, (CAP, n_tok)) > 0.5,
        ),
        1.0,
        0.0,
    ).astype(F32)
    sel_b = sel.astype(BF)
    xs[0:CAP, :] = dot(sel_b, tokens[...]).astype(BF)
    ds[0:CAP, 0:D] = dot(sel_b, out_grad[...]).astype(BF)
    w_own = jnp.sum(sel * prob[...].astype(F32), axis=1, keepdims=True)
    ds[0:CAP, D:] = jnp.broadcast_to(w_own, (CAP, 128)).astype(BF)

    pl.semaphore_wait(barrier, len(dev))

    arriving = {}

    def gsend(name, key, to, parts="xd"):
        a, b = pl.ds(SLOT[key] * CAP, CAP), pl.ds(SLOT[to] * CAP, CAP)
        for part in parts:
            buf = xs if part == "x" else ds
            arriving[to + (part,)] = send(name, buf.at[a, :], buf.at[b, :])

    def gwait(*keys, parts="xd"):
        for key in keys:
            for part in parts:
                arriving[key + (part,)].wait_recv()

    def compute(g):
        rows = slice(g * 128, (g + 1) * 128)
        wcol = ds[rows, D:].astype(F32)[:, 0:1]
        n_f = 2
        fw = F // n_f
        psum = jnp.zeros((128, 1), F32)
        for f in range(n_f):
            cols = slice(f * fw, (f + 1) * fw)
            gate = dot(xs[rows, :], wg[:, cols])
            up = dot(xs[rows, :], wu[:, cols])
            raw = dot_t(ds[rows, 0:D], wd[cols, :])
            sig = 1.0 / (1.0 + jnp.exp(-gate))
            act = gate * sig
            hid = (act * up).astype(BF).astype(F32)
            gh = wcol * raw
            gs[2, rows, cols] = (wcol * hid).astype(BF)
            gs[0, rows, cols] = (gh * up * sig * (1.0 + gate * (1.0 - sig))).astype(BF)
            gs[1, rows, cols] = (gh * act).astype(BF)
            psum = psum + jnp.sum(hid * raw, axis=1, keepdims=True)
        pbr = jnp.broadcast_to(psum, (128, 128))
        for q in range(4):
            r = pair_row(*ORDER[4 * g + q])
            pb[r : r + CAP, :] = pbr[q * CAP : (q + 1) * CAP, :]

        def tok_tile(n, carry):
            at = pl.multiple_of(n * 512, 512)
            t = (
                dot_t(gs[0, rows, :], wg[pl.ds(at, 512), :])
                + dot_t(gs[1, rows, :], wu[pl.ds(at, 512), :])
            ).astype(BF)
            for q in range(4):
                r = pair_row(*ORDER[4 * g + q])
                tp[r : r + CAP, pl.ds(at, 512)] = t[q * CAP : (q + 1) * CAP, :]
            return carry

        lax.fori_loop(0, D // 512, tok_tile, 0)

        def turn(n, carry):
            at = pl.multiple_of(n * 256, 256)
            xt[pl.ds(at, 256), rows] = xs[rows, pl.ds(at, 256)].T
            dt[pl.ds(at, 256), rows] = ds[rows, pl.ds(at, 256)].T
            return carry

        lax.fori_loop(0, D // 256, turn, 0)

    for name in ("z+", "z-", "yl"):
        gsend(name, (0, 0), {"z+": (0, 1), "z-": (0, -1), "yl": (1, 0)}[name])
    for cp in loads:
        cp.wait()
    gwait((0, 1))
    gsend("z+", (0, 1), (0, 2))
    gwait((0, -1))
    gsend("z-", (0, -1), (0, -2))
    gwait((1, 0))
    gsend("yl", (0, 1), (1, 1))
    gsend("yl", (0, -1), (1, -1))
    compute(0)
    gwait((0, 2))
    gsend("z+", (0, 2), (0, 3))
    gwait((0, -2))
    gsend("z-", (0, -2), (0, -3))
    gwait((1, 1), (1, -1))
    gsend("yl", (0, 2), (1, 2), "x")
    gsend("yl", (0, -2), (1, -2), "x")
    gwait((0, 3))
    gsend("z+", (0, 3), (0, 4), "x")
    gsend("z+", (1, 1), (1, 2), "d")
    gwait((0, -3))
    gsend("z-", (0, -3), (0, 4), "d")
    gsend("z-", (1, -1), (1, -2), "d")
    compute(1)
    gwait((0, 4))
    gsend("yl", (0, 4), (1, 4))
    gwait((1, 2))
    gsend("z+", (1, 2), (1, 3))
    gwait((1, -2))
    gsend("z-", (1, -2), (1, -3))
    compute(2)
    gwait((1, 3), (1, -3), (1, 4))
    compute(3)

    def add_rows(dst, dst_row, src, src_row, n, cols):
        def body(i, carry):
            a = pl.ds(pl.multiple_of(dst_row + i * 16, 16), 16)
            b = pl.ds(pl.multiple_of(src_row + i * 16, 16), 16)
            dst[a, cols] = (dst[a, cols].astype(F32) + src[b, :].astype(F32)).astype(BF)
            return carry

        lax.fori_loop(0, n // 16, body, 0)

    chain = {"z+": {}, "z-": {}}
    PAIR = 2 * CAP
    side = {"z+": 0, "z-": 1}

    def tok_step(k):
        for name, sign in (("z+", -1), ("z-", 1)):
            i = side[name]
            r = pair_row(0, sign * k)
            if k == 4:
                cols = slice(0, H) if i == 0 else slice(H, D)
                got = send(name, tp.at[pl.ds(r, PAIR), cols], rph.at[i])
                gotp = None
                if i == 0:
                    gotp = send(name, pb.at[pl.ds(r, PAIR), :], pr.at[i, 0])
            else:
                before_t, before_p = chain[name][k + 1]
                before_t.wait_recv()
                if k == 3:
                    cols = slice(0, H) if i == 0 else slice(H, D)
                    add_rows(tp, r, rph.at[i], 0, PAIR, cols)
                else:
                    add_rows(tp, r, rp.at[i, 2 - k], 0, PAIR, slice(0, D))
                if before_p is not None:
                    before_p.wait_recv()
                    pb[r : r + PAIR, :] = pb[r : r + PAIR, :] + pr[i, 3 - k]
                got = send(name, tp.at[pl.ds(r, PAIR), :], rp.at[i, 3 - k])
                gotp = send(name, pb.at[pl.ds(r, PAIR), :], pr.at[i, 4 - k])
            chain[name][k] = (got, gotp)

    def tok_sum():
        for name in ("z+", "z-"):
            chain[name][1][0].wait_recv()
            chain[name][1][1].wait_recv()
        a = slice(CAP, PAIR)
        tp[a, :] = (
            tp[a, :].astype(F32) + rp[0, 2, a, :].astype(F32) + rp[1, 2, a, :].astype(F32)
        ).astype(BF)
        pb[a, :] = pb[a, :] + pr[0, 3, a, :] + pr[1, 3, a, :]
        t = send("yl", tp.at[pl.ds(CAP, CAP), :], ry)
        p = send("yl", pb.at[pl.ds(CAP, CAP), :], pry)
        return t, p

    def tok_final(t, p):
        t.wait_recv()
        a = slice(0, CAP)
        total = (
            tp[a, :].astype(F32) + rp[0, 2, a, :].astype(F32) + rp[1, 2, a, :].astype(F32)
            + ry[...].astype(F32)
        ).astype(BF)
        o_tok[...] = dot(sel.T.astype(BF), total).astype(BF)
        p.wait_recv()
        psum = pb[a, :] + pr[0, 3, a, :] + pr[1, 3, a, :] + pry[...]
        o_prob[...] = jnp.sum(sel * psum, axis=0, keepdims=True)

    def chunk_dot(key, pc, p):
        dx, h = key
        owner = dp_of((x + dx + 4) % 4, (yh + h) % 2, pc)
        at = pl.multiple_of(owner * rows_own, 64)
        lhs = dt if p == 2 else xt
        return dot(lhs[pl.ds(at, rows_own), :], gs[p])

    tok_step(4)
    from_core = []
    for i, key in enumerate(CHUNKS):
        for p in range(3):
            ws[i, p] = chunk_dot(key, 1 - core, p).astype(BF)
        from_core.append(send("c", ws.at[i], sr.at[i]))

    def own_chunk(key):
        i = CIDX[key]
        from_core[i].wait_recv()
        for p in range(3):
            sr[i, p] = (chunk_dot(key, core, p) + sr[i, p].astype(F32)).astype(BF)

    far = {}

    def far_send(h):
        i = CIDX[(2, h)]
        for s, name in ((0, "x+"), (1, "x-")):
            far[name, h] = send(name, sr.at[i, :, pl.ds(s * half, half), :], xa.at[s, h])

    near = {}

    def near_add(h):
        for s, name, dx in ((0, "x+", 1), (1, "x-", -1)):
            far[name, h].wait_recv()
            i = CIDX[(dx, h)]
            r = slice(s * half, (s + 1) * half)
            for p in range(3):
                sr[i, p, r, :] = (sr[i, p, r, :].astype(F32) + xa[s, h, p].astype(F32)).astype(BF)

    def near_send(h, p):
        for s, name, dx in ((0, "x+", 1), (1, "x-", -1)):
            near[name, h, p] = send(name, sr.at[CIDX[(dx, h)], p], xb.at[s, h, p])

    def near_wait(h, p):
        for name in ("x+", "x-"):
            near[name, h, p].wait_recv()

    to_y = {}

    own_chunk((2, 1))
    far_send(1)
    own_chunk((2, 0))
    far_send(0)
    own_chunk((1, 1))
    own_chunk((-1, 1))
    tok_step(3)
    near_add(1)
    for p in range(3):
        near_send(1, p)
    own_chunk((1, 0))
    own_chunk((-1, 0))
    own_chunk((0, 1))
    own_chunk((0, 0))
    tok_step(2)
    near_add(0)
    tok_step(1)

    def y_send(p):
        near_wait(1, p)
        i = CIDX[(0, 1)]
        sr[i, p] = (
            sr[i, p].astype(F32) + xb[0, 1, p].astype(F32) + xb[1, 1, p].astype(F32)
        ).astype(BF)
        to_y[p] = send("y2", sr.at[i, p], yb.at[p])

    for p in range(3):
        y_send(p)
        near_send(0, p)
    t, q = tok_sum()
    tok_final(t, q)
    i = CIDX[(0, 0)]
    for p in range(3):
        near_wait(0, p)
        to_y[p].wait_recv()
        o_w[p] = (
            (
                sr[i, p].astype(F32) + xb[0, 0, p].astype(F32) + xb[1, 0, p].astype(F32)
                + yb[p].astype(F32)
            )
            * (1.0 / 16.0)
        ).astype(BF)
    for cp in sent:
        cp.wait_send()


def shards(tokens, out_grad, route_ids, route_prob, w_gate, w_up, w_down):
    n_tok, D = tokens.shape
    F = w_gate.shape[1]
    own = D // lax.axis_size("dp")
    rows = CAP * lax.axis_size("etp")
    vmem = pl.BlockSpec(memory_space=pltpu.VMEM)
    hbm = pl.BlockSpec(memory_space=pl.ANY)
    n_sem = 100
    scratch = [
        pltpu.VMEM((D, F), BF),
        pltpu.VMEM((D, F), BF),
        pltpu.VMEM((F, D), BF),
        pltpu.VMEM((rows, D), BF),
        pltpu.VMEM((rows, D + 128), BF),
        pltpu.VMEM((D, rows), BF),
        pltpu.VMEM((D, rows), BF),
        pltpu.VMEM((3, rows, F), BF),
        pltpu.VMEM((rows, D), BF),
        pltpu.VMEM((rows, 128), F32),
        pltpu.VMEM((8, 3, own, F), BF),
        pltpu.VMEM((8, 3, own, F), BF),
        pltpu.VMEM((2, 2, 3, own // 2, F), BF),
        pltpu.VMEM((2, 2, 3, own, F), BF),
        pltpu.VMEM((3, own, F), BF),
        pltpu.VMEM((2, 3, 2 * CAP, D), BF),
        pltpu.VMEM((2, 2 * CAP, D // 2), BF),
        pltpu.VMEM((2, 4, 2 * CAP, 128), F32),
        pltpu.VMEM((CAP, D), BF),
        pltpu.VMEM((CAP, 128), F32),
        pltpu.SemaphoreType.DMA((3,)),
        pltpu.SemaphoreType.DMA((n_sem,)),
        pltpu.SemaphoreType.DMA((n_sem,)),
    ]
    g_tok, g_prob, g_w = pl.pallas_call(
        kernel,
        out_shape=(
            jax.ShapeDtypeStruct((n_tok, D), BF),
            jax.ShapeDtypeStruct((1, n_tok), F32),
            jax.ShapeDtypeStruct((3, own, F), BF),
        ),
        in_specs=[vmem] * 4 + [hbm] * 3,
        out_specs=(vmem, vmem, vmem),
        scratch_shapes=scratch,
        compiler_params=pltpu.CompilerParams(
            collective_id=0, has_side_effects=True, vmem_limit_bytes=60 * 1024 * 1024
        ),
        cost_estimate=pl.CostEstimate(
            flops=8 * 2 * rows * D * F, bytes_accessed=6 * D * F + 8 * n_tok * D, transcendentals=rows * F
        ),
    )(route_ids.T, route_prob.reshape(1, n_tok), tokens, out_grad, w_gate, w_up, w_down)
    return g_tok, g_prob.reshape(n_tok), g_w[0], g_w[1], g_w[2].T


def solution(mesh):
    placed = (
        P(("dp", "etp"), None),
        P(("dp", "etp"), None),
        P(("dp", "etp"), None),
        P(("dp", "etp")),
        P(None, "etp"),
        P(None, "etp"),
        P("etp", None),
    )
    return jax.shard_map(
        shards,
        mesh=mesh,
        in_specs=placed,
        out_specs=(
            P(("dp", "etp"), None),
            P(("dp", "etp")),
            P("dp", "etp"),
            P("dp", "etp"),
            P("etp", "dp"),
        ),
        check_vma=False,
    )
```

```python
import functools

import jax
import jax.numpy as jnp
from jax import lax
from jax.experimental import pallas as pl
from jax.experimental.pallas import tpu as pltpu
from jax.sharding import PartitionSpec as P

MESH = pl.DeviceIdType.MESH
CAP = 32
BF = jnp.bfloat16
F32 = jnp.float32

ORDER = (
    (0, 0), (1, 0), (0, 1), (0, -1),
    (0, 2), (0, -2), (1, 1), (1, -1),
    (0, 3), (0, -3), (0, 4), (1, 2),
    (1, -2), (1, 3), (1, -3), (1, 4),
)
SLOT = {key: i for i, key in enumerate(ORDER)}
CHUNKS = ((2, 0), (2, 1), (1, 0), (1, 1), (-1, 0), (-1, 1), (0, 0), (0, 1))
CIDX = {key: i for i, key in enumerate(CHUNKS)}


def pair_row(col, off):
    return ((off % 8) * 2 + col) * CAP


def dot(a, b):
    return jnp.dot(a, b, preferred_element_type=F32)


def dot_t(a, b):
    return lax.dot_general(a, b, (((1,), (1,)), ((), ())), preferred_element_type=F32)


def routed_rows(ids):
    routed = jnp.logical_or(ids[0:1, :] == 0, ids[1:2, :] == 0)
    n_tok = routed.shape[1]
    routed_f = jnp.where(routed, 1.0, 0.0).astype(F32)
    before = (
        lax.broadcasted_iota(jnp.int32, (n_tok, n_tok), 0)
        < lax.broadcasted_iota(jnp.int32, (n_tok, n_tok), 1)
    )
    rank = dot(
        jnp.broadcast_to(routed_f, (16, n_tok)).astype(BF),
        jnp.where(before, 1.0, 0.0).astype(BF),
    )[0:1, :]
    slot_no = lax.broadcasted_iota(jnp.int32, (CAP, n_tok), 0).astype(F32)
    chosen = jnp.logical_and(
        jnp.broadcast_to(rank, (CAP, n_tok)) == slot_no,
        jnp.broadcast_to(routed_f, (CAP, n_tok)) > 0.5,
    )
    return jnp.where(chosen, 1.0, 0.0).astype(F32)


def kernel(
    ids, prob, tokens_h, out_grad_h, w_gate_h, w_up_h, w_down_h,
    o_tok, o_prob, o_w,
    tokens, out_grad, wg, wu, wd, wgt, wut, xs, ds, xt, dt, gs, tp, pb, ws, sr, xa, xb, yb, yc,
    rp, rph, pr, ry, pry, fw,
    w_sem, o_sem, s_sem, r_sem,
):
    D = xs.shape[1]
    F = wg.shape[1]
    H = D // 2
    rows_own = fw.shape[1]
    half = rows_own // 2
    dp, etp = lax.axis_index("dp"), lax.axis_index("etp")
    x, yh, core = dp // 4, (dp // 2) % 2, dp % 2
    z, yl = etp // 2, etp % 2

    def dp_of(px, ph, pc):
        return px * 4 + ph * 2 + pc

    dev = {
        "z+": (dp, ((z + 1) % 8) * 2 + yl),
        "z-": (dp, ((z + 7) % 8) * 2 + yl),
        "yl": (dp, z * 2 + 1 - yl),
        "x+": (dp_of((x + 1) % 4, yh, core), etp),
        "x-": (dp_of((x + 3) % 4, yh, core), etp),
        "y2": (dp_of(x, 1 - yh, core), etp),
        "c": (dp_of(x, yh, 1 - core), etp),
    }
    barrier = pltpu.get_barrier_semaphore()
    for name in dev:
        pl.semaphore_signal(barrier, inc=1, device_id=dev[name], device_id_type=MESH)

    loads = []

    def load(src, dst):
        cp = pltpu.make_async_copy(src, dst, w_sem.at[len(loads)])
        cp.start()
        loads.append(cp)

    load(tokens_h, tokens)
    load(out_grad_h, out_grad)

    count = [0]
    sent, free = [], list(range(s_sem.shape[0]))

    def drain():
        for cp, k in sent:
            cp.wait_send()
            free.append(k)
        sent.clear()

    def send(name, src, dst):
        i, k = count[0], free.pop(0)
        count[0] += 1
        cp = pltpu.make_async_remote_copy(
            src_ref=src, dst_ref=dst, send_sem=s_sem.at[k], recv_sem=r_sem.at[i],
            device_id=dev[name], device_id_type=MESH,
        )
        cp.start()
        sent.append((cp, k))
        return cp

    with jax.named_scope("pack"):
        sel = routed_rows(ids)
        sel_b = sel.astype(BF)
        w_own = jnp.sum(sel * prob[...].astype(F32), axis=1, keepdims=True)
        ds[0:CAP, D:] = jnp.broadcast_to(w_own, (CAP, 128)).astype(BF)
        loads[0].wait()
        xs[0:CAP, :] = dot(sel_b, tokens[...]).astype(BF)
        loads[1].wait()
        ds[0:CAP, 0:D] = dot(sel_b, out_grad[...]).astype(BF)
        load(w_gate_h, wg)
        load(w_up_h, wu)
        load(w_down_h, wd)

    with jax.named_scope("barrier_wait"):
        pl.semaphore_wait(barrier, len(dev))

    arriving = {}

    def gsend(name, key, to, parts="xd"):
        a, b = pl.ds(SLOT[key] * CAP, CAP), pl.ds(SLOT[to] * CAP, CAP)
        for part in parts:
            buf = xs if part == "x" else ds
            arriving[to + (part,)] = send(name, buf.at[a, :], buf.at[b, :])

    def gwait(*keys, parts="xd"):
        for key in keys:
            for part in parts:
                arriving[key + (part,)].wait_recv()

    def forward(g):
        rows = slice(g * 128, (g + 1) * 128)
        wcol = ds[rows, D:].astype(F32)[:, 0:1]
        n_f = 2
        fw_ = F // n_f
        psum = jnp.zeros((128, 1), F32)
        for f in range(n_f):
            cols = slice(f * fw_, (f + 1) * fw_)
            gate = dot(xs[rows, :], wg[:, cols])
            up = dot(xs[rows, :], wu[:, cols])
            raw = dot_t(ds[rows, 0:D], wd[cols, :])
            sig = 1.0 / (1.0 + jnp.exp(-gate))
            act = gate * sig
            hid = (act * up).astype(BF).astype(F32)
            gh = wcol * raw
            gs[2, rows, cols] = (wcol * hid).astype(BF)
            gs[0, rows, cols] = (gh * up * sig * (1.0 + gate * (1.0 - sig))).astype(BF)
            gs[1, rows, cols] = (gh * act).astype(BF)
            psum = psum + jnp.sum(hid * raw, axis=1, keepdims=True)
        pbr = jnp.broadcast_to(psum, (128, 128))
        for q in range(4):
            r = pair_row(*ORDER[4 * g + q])
            pb[r : r + CAP, :] = pbr[q * CAP : (q + 1) * CAP, :]

    def token_part(g):
        rows = slice(g * 128, (g + 1) * 128)

        def tok_tile(n, carry):
            at = pl.multiple_of(n * 512, 512)
            t = (
                dot(gs[0, rows, :], wgt[:, pl.ds(at, 512)])
                + dot(gs[1, rows, :], wut[:, pl.ds(at, 512)])
            ).astype(BF)
            for q in range(4):
                r = pair_row(*ORDER[4 * g + q])
                tp[r : r + CAP, pl.ds(at, 512)] = t[q * CAP : (q + 1) * CAP, :]
            return carry

        lax.fori_loop(0, D // 512, tok_tile, 0)

    def turn(g, src, dst):
        rows = slice(g * 128, (g + 1) * 128)

        def body(n, carry):
            at = pl.multiple_of(n * 256, 256)
            dst[pl.ds(at, 256), rows] = src[rows, pl.ds(at, 256)].T
            return carry

        lax.fori_loop(0, D // 256, body, 0)

    def compute(g):
        with jax.named_scope("forward_g%d" % g):
            forward(g)
        with jax.named_scope("token_g%d" % g):
            token_part(g)
        with jax.named_scope("turn_g%d" % g):
            turn(g, xs, xt)
            turn(g, ds, dt)

    def add_rows(dst, dst_row, src, n, cols):
        def body(i, carry):
            a = pl.ds(pl.multiple_of(dst_row + i * 16, 16), 16)
            b = pl.ds(pl.multiple_of(i * 16, 16), 16)
            dst[a, cols] = (dst[a, cols].astype(F32) + src[b, :].astype(F32)).astype(BF)
            return carry

        lax.fori_loop(0, n // 16, body, 0)

    chain = {}

    def tok_step(c, k):
        for i, name, sign in ((0, "z+", -1), (1, "z-", 1)):
            r = pair_row(c, sign * k)
            mine = pl.ds(r, CAP)
            pair = pair_row(0, sign * k)
            both = slice(pair, pair + 2 * CAP)
            gotp = None
            if k == 4:
                cols = slice(0, H) if i == 0 else slice(H, D)
                got = send(name, tp.at[mine, cols], rph.at[i, c])
                if c == 1 and i == 0:
                    gotp = send(name, pb.at[both, :], pr.at[i, 0])
            else:
                before_t, before_p = chain[name, c, k + 1]
                before_t.wait_recv()
                if k == 3:
                    cols = slice(0, H) if i == 0 else slice(H, D)
                    add_rows(tp, r, rph.at[i, c], CAP, cols)
                else:
                    add_rows(tp, r, rp.at[i, c, 2 - k], CAP, slice(0, D))
                got = send(name, tp.at[mine, :], rp.at[i, c, 3 - k])
                if c == 1:
                    if before_p is not None:
                        before_p.wait_recv()
                        pb[both, :] = pb[both, :] + pr[i, 3 - k]
                    gotp = send(name, pb.at[both, :], pr.at[i, 4 - k])
            chain[name, c, k] = (got, gotp)

    def tok_arrived(c):
        for name in ("z+", "z-"):
            for cp in chain[name, c, 1]:
                if cp is not None:
                    cp.wait_recv()

    own_rows, other_rows = slice(0, CAP), slice(CAP, 2 * CAP)

    def tok_cross():
        tok_arrived(1)

        def body(i, carry):
            a = pl.ds(pl.multiple_of(CAP + i * 16, 16), 16)
            b = pl.ds(pl.multiple_of(i * 16, 16), 16)
            tp[a, :] = (
                tp[a, :].astype(F32) + rp[0, 1, 2, b, :].astype(F32) + rp[1, 1, 2, b, :].astype(F32)
            ).astype(BF)
            return carry

        lax.fori_loop(0, CAP // 16, body, 0)
        t = send("yl", tp.at[pl.ds(CAP, CAP), :], ry)
        pb[other_rows, :] = pb[other_rows, :] + pr[0, 3, other_rows] + pr[1, 3, other_rows]
        p = send("yl", pb.at[pl.ds(CAP, CAP), :], pry)
        return t, p

    def tok_final(t, p):
        tok_arrived(0)
        t.wait_recv()
        p.wait_recv()

        def body(i, carry):
            a = pl.ds(pl.multiple_of(i * 16, 16), 16)
            ry[a, :] = (
                tp[a, :].astype(F32) + rp[0, 0, 2, a, :].astype(F32)
                + rp[1, 0, 2, a, :].astype(F32) + ry[a, :].astype(F32)
            ).astype(BF)
            return carry

        lax.fori_loop(0, CAP // 16, body, 0)
        pry[...] = pb[own_rows, :] + pr[0, 3, own_rows] + pr[1, 3, own_rows] + pry[...]
        out(0, ry, o_tok)
        out(1, pry, o_prob)

    outs = []

    def out(i, src, dst):
        cp = pltpu.make_async_copy(src, dst, o_sem.at[i])
        cp.start()
        outs.append(cp)

    def chunk_dot(key, pc, p):
        dx, h = key
        owner = dp_of((x + dx + 4) % 4, (yh + h) % 2, pc)
        at = pl.multiple_of(owner * rows_own, 64)
        lhs = dt if p == 2 else xt
        return dot(lhs[pl.ds(at, rows_own), :], gs[p])

    from_core = {}
    met = set()

    def sib(p, *keys):
        for key in keys:
            ws[p, CIDX[key]] = chunk_dot(key, 1 - core, p).astype(BF)
        at = pl.ds(CIDX[keys[0]], len(keys))
        cp = send("c", ws.at[p, at], sr.at[p, at])
        for key in keys:
            from_core[key, p] = cp

    def own(p, *keys):
        for key in keys:
            i = CIDX[key]
            v = chunk_dot(key, core, p)
            cp = from_core[key, p]
            if id(cp) not in met:
                met.add(id(cp))
                cp.wait_recv()
            sr[p, i] = (v + sr[p, i].astype(F32)).astype(BF)

    far = {}

    def far_send(h, p):
        i = CIDX[(2, h)]
        for s, name in ((0, "x+"), (1, "x-")):
            far[name, h, p] = send(name, sr.at[p, i, pl.ds(s * half, half), :], xa.at[s, h, p])

    near = {}

    def near_send(h, p):
        for s, name, dx in ((0, "x+", 1), (1, "x-", -1)):
            far[name, h, p].wait_recv()
            i = CIDX[(dx, h)]
            r = slice(s * half, (s + 1) * half)
            sr[p, i, r, :] = (sr[p, i, r, :].astype(F32) + xa[s, h, p].astype(F32)).astype(BF)
            near[name, h, p] = send(name, sr.at[p, i], xb.at[s, h, p])

    def near_wait(h, p):
        for name in ("x+", "x-"):
            near[name, h, p].wait_recv()

    to_y = {}

    def y_last(p):
        near_wait(1, p)
        i = CIDX[(0, 1)]
        sr[p, i] = (
            sr[p, i].astype(F32) + xb[0, 1, p].astype(F32) + xb[1, 1, p].astype(F32)
        ).astype(BF)
        to_y[p] = send("y2", sr.at[p, i], yb.at[p])

    def y_first(dx):
        to_y[2, dx] = send("y2", sr.at[2, CIDX[(dx, 1)]], yc.at[CIDX[(dx, 0)] // 2])

    def y_add(dx):
        to_y[2, dx].wait_recv()
        i = CIDX[(dx, 0)]
        sr[2, i] = (sr[2, i].astype(F32) + yc[i // 2].astype(F32)).astype(BF)

    def w_final(p):
        near_wait(0, p)
        i = CIDX[(0, 0)]
        total = sr[p, i].astype(F32) + xb[0, 0, p].astype(F32) + xb[1, 0, p].astype(F32)
        if p < 2:
            to_y[p].wait_recv()
            total = total + yb[p].astype(F32)
        fw[p] = (total * (1.0 / 16.0)).astype(BF)
        out(2 + p, fw.at[p], o_w.at[p])

    scope = jax.named_scope

    gsend("z+", (0, 0), (0, 1))
    gsend("z-", (0, 0), (0, -1))
    gsend("yl", (0, 0), (1, 0))
    with scope("wait_weights"):
        for cp in loads[2:]:
            cp.wait()
    with scope("turn_weights"):
        def turn_weights(n, carry):
            at = pl.multiple_of(n * 256, 256)
            wgt[:, pl.ds(at, 256)] = wg[pl.ds(at, 256), :].T
            wut[:, pl.ds(at, 256)] = wu[pl.ds(at, 256), :].T
            return carry

        lax.fori_loop(0, D // 256, turn_weights, 0)
    with scope("wait_1"):
        for part in "xd":
            gwait((0, 1), parts=part)
            gsend("z+", (0, 1), (0, 2), part)
            gsend("yl", (0, 1), (1, 1), part)
            gwait((0, -1), parts=part)
            gsend("z-", (0, -1), (0, -2), part)
            gsend("yl", (0, -1), (1, -1), part)
        gwait((1, 0))
    compute(0)
    with scope("wait_2"):
        for part in "xd":
            gwait((0, 2), parts=part)
            gsend("z+", (0, 2), (0, 3), part)
            gwait((0, -2), parts=part)
            gsend("z-", (0, -2), (0, -3), part)
    with scope("wait_y_x"):
        gwait((1, 1), (1, -1), parts="x")
        gsend("yl", (0, 2), (1, 2), "x")
        gsend("yl", (0, -2), (1, -2), "x")
    with scope("wait_3"):
        gwait((0, 3), parts="x")
        gsend("z+", (0, 3), (0, 4), "x")
        gwait((0, -3), parts="d")
        gsend("z-", (0, -3), (0, 4), "d")
        gwait((1, 1), parts="d")
        gsend("z+", (1, 1), (1, 2), "d")
        gwait((1, -1), parts="d")
        gsend("z-", (1, -1), (1, -2), "d")
    compute(1)
    with scope("wait_4"):
        gwait((0, 4))
        gsend("yl", (0, 4), (1, 4))
    with scope("wait_5"):
        for part in "xd":
            gwait((1, 2), parts=part)
            gsend("z+", (1, 2), (1, 3), part)
            gwait((1, -2), parts=part)
            gsend("z-", (1, -2), (1, -3), part)
        gwait((0, 3), parts="d")
        gwait((0, -3), parts="x")
    compute(2)
    with scope("wait_6x"):
        gwait((1, 3), (1, -3), (1, 4), parts="x")
    with scope("turn_x"):
        turn(3, xs, xt)
    with scope("wait_6d"):
        gwait((1, 3), (1, -3), (1, 4), parts="d")
    with scope("forward_g3"):
        forward(3)
    with scope("drain_gather"):
        drain()
    tok_step(0, 4)
    with scope("chunks_a"):
        sib(0, (2, 0), (2, 1))
        turn(3, ds, dt)
        sib(2, (2, 1))
        sib(2, (1, 1))
        own(0, (2, 1))
        far_send(1, 0)
        own(0, (2, 0))
        far_send(0, 0)
        own(2, (2, 1))
        y_first(2)
        own(2, (1, 1))
        y_first(1)
    with scope("tok_0_3"):
        tok_step(0, 3)
    with scope("token_g3"):
        token_part(3)
    tok_step(1, 4)
    with scope("chunks_b"):
        sib(1, (2, 0), (2, 1))
        sib(0, (1, 0), (1, 1), (-1, 0), (-1, 1))
        sib(2, (-1, 1))
        sib(2, (0, 1))
        own(1, (2, 1))
        far_send(1, 1)
        own(1, (2, 0))
        far_send(0, 1)
        own(0, (1, 1), (-1, 1))
    with scope("near_h1_p0"):
        near_send(1, 0)
    with scope("tok_0_2"):
        own(0, (1, 0), (-1, 0))
        tok_step(0, 2)
    with scope("near_h0_p0"):
        near_send(0, 0)
    with scope("y_first_rest"):
        own(2, (-1, 1))
        y_first(-1)
        own(2, (0, 1))
        y_first(0)
    with scope("tok_1_3"):
        tok_step(1, 3)
    with scope("chunks_c"):
        sib(1, (1, 0), (1, 1), (-1, 0), (-1, 1))
        sib(2, (2, 0))
        sib(2, (1, 0))
        sib(2, (-1, 0))
        sib(0, (0, 0), (0, 1))
        sib(1, (0, 0), (0, 1))
        sib(2, (0, 0))
        own(2, (2, 0))
    with scope("y_add_2"):
        y_add(2)
        far_send(0, 2)
    with scope("chunks_d"):
        own(1, (1, 1), (-1, 1), (1, 0), (-1, 0))
    with scope("near_h1_p1"):
        near_send(1, 1)
    with scope("near_h0_p1"):
        near_send(0, 1)
    with scope("chunks_e"):
        own(2, (1, 0), (-1, 0), (0, 0))
        own(0, (0, 1), (0, 0))
        own(1, (0, 1), (0, 0))
    with scope("tok_0_1"):
        tok_step(0, 1)
    with scope("tok_1_2"):
        tok_step(1, 2)
    with scope("y_add_near"):
        y_add(1)
        y_add(-1)
    with scope("near_h0_p2"):
        near_send(0, 2)
    with scope("y_last_0"):
        y_last(0)
    with scope("y_add_0"):
        y_add(0)
    with scope("tok_1_1"):
        tok_step(1, 1)
    with scope("y_last_1"):
        y_last(1)
    with scope("tok_cross"):
        t, q = tok_cross()
    with scope("w_final_0"):
        w_final(0)
    with scope("w_final_1"):
        w_final(1)
    with scope("w_final_2"):
        w_final(2)
    with scope("tok_final"):
        tok_final(t, q)
    with scope("drain"):
        drain()
        for cp in outs:
            cp.wait()


def finish(ids, packed, psum, w_in, o_tok, o_prob, o_gate, o_up, o_down):
    sel = routed_rows(ids)
    o_gate[...] = w_in[0]
    o_up[...] = w_in[1]
    o_down[...] = w_in[2]
    o_tok[...] = dot(sel.T.astype(BF), packed[...]).astype(BF)
    o_prob[...] = jnp.sum(sel * psum[...], axis=0, keepdims=True)


def shards(tokens, out_grad, route_ids, route_prob, w_gate, w_up, w_down):
    n_tok, D = tokens.shape
    F = w_gate.shape[1]
    own = D // lax.axis_size("dp")
    rows = CAP * lax.axis_size("etp")
    vmem = pl.BlockSpec(memory_space=pltpu.VMEM)
    hbm = pl.BlockSpec(memory_space=pl.ANY)
    n_send, n_recv = 65, 95
    scratch = [
        pltpu.VMEM((n_tok, D), BF),
        pltpu.VMEM((n_tok, D), BF),
        pltpu.VMEM((D, F), BF),
        pltpu.VMEM((D, F), BF),
        pltpu.VMEM((F, D), BF),
        pltpu.VMEM((F, D), BF),
        pltpu.VMEM((F, D), BF),
        pltpu.VMEM((rows, D), BF),
        pltpu.VMEM((rows, D + 128), BF),
        pltpu.VMEM((D, rows), BF),
        pltpu.VMEM((D, rows), BF),
        pltpu.VMEM((3, rows, F), BF),
        pltpu.VMEM((rows, D), BF),
        pltpu.VMEM((rows, 128), F32),
        pltpu.VMEM((3, 8, own, F), BF),
        pltpu.VMEM((3, 8, own, F), BF),
        pltpu.VMEM((2, 2, 3, own // 2, F), BF),
        pltpu.VMEM((2, 2, 3, own, F), BF),
        pltpu.VMEM((2, own, F), BF),
        pltpu.VMEM((4, own, F), BF),
        pltpu.VMEM((2, 2, 3, CAP, D), BF),
        pltpu.VMEM((2, 2, CAP, D // 2), BF),
        pltpu.VMEM((2, 4, 2 * CAP, 128), F32),
        pltpu.VMEM((CAP, D), BF),
        pltpu.VMEM((CAP, 128), F32),
        pltpu.VMEM((3, own, F), BF),
        pltpu.SemaphoreType.DMA((5,)),
        pltpu.SemaphoreType.DMA((5,)),
        pltpu.SemaphoreType.DMA((n_send,)),
        pltpu.SemaphoreType.DMA((n_recv,)),
    ]
    ids = route_ids.T
    packed, psum, g_w = pl.pallas_call(
        kernel,
        out_shape=(
            jax.ShapeDtypeStruct((CAP, D), BF),
            jax.ShapeDtypeStruct((CAP, 128), F32),
            jax.ShapeDtypeStruct((3, own, F), BF),
        ),
        in_specs=[vmem] * 2 + [hbm] * 5,
        out_specs=(hbm, hbm, hbm),
        scratch_shapes=scratch,
        compiler_params=pltpu.CompilerParams(
            collective_id=0, has_side_effects=True, vmem_limit_bytes=60 * 1024 * 1024
        ),
        cost_estimate=pl.CostEstimate(
            flops=8 * 2 * rows * D * F, bytes_accessed=6 * D * F + 8 * n_tok * D, transcendentals=rows * F
        ),
    )(ids, route_prob.reshape(1, n_tok), tokens, out_grad, w_gate, w_up, w_down)
    g_tok, g_prob, g_gate, g_up, g_down = pl.pallas_call(
        finish,
        out_shape=(
            jax.ShapeDtypeStruct((n_tok, D), BF),
            jax.ShapeDtypeStruct((1, n_tok), F32),
        )
        + (jax.ShapeDtypeStruct((own, F), BF),) * 3,
        in_specs=[vmem] * 4,
        out_specs=(vmem,) * 5,
    )(ids, packed, psum, g_w)
    return g_tok, g_prob.reshape(n_tok), g_gate, g_up, g_down.T


def solution(mesh):
    placed = (
        P(("dp", "etp"), None),
        P(("dp", "etp"), None),
        P(("dp", "etp"), None),
        P(("dp", "etp")),
        P(None, "etp"),
        P(None, "etp"),
        P("etp", None),
    )
    return jax.shard_map(
        shards,
        mesh=mesh,
        in_specs=placed,
        out_specs=(
            P(("dp", "etp"), None),
            P(("dp", "etp")),
            P("dp", "etp"),
            P("dp", "etp"),
            P("etp", "dp"),
        ),
        check_vma=False,
    )
```

```python
import functools

import jax
import jax.numpy as jnp
from jax import lax
from jax.experimental import pallas as pl
from jax.experimental.pallas import tpu as pltpu
from jax.sharding import PartitionSpec as P

MESH = pl.DeviceIdType.MESH
CAP = 32
BF = jnp.bfloat16
F32 = jnp.float32

ORDER = (
    (0, 0), (1, 0), (0, 1), (0, -1),
    (0, 2), (0, -2), (1, 1), (1, -1),
    (0, 3), (0, -3), (1, 2), (1, -2),
    (0, 4), (1, 3), (1, -3), (1, 4),
)
HALF = CAP // 2
SLOT = {key: i for i, key in enumerate(ORDER)}
CHUNKS = ((2, 0), (2, 1), (1, 0), (1, 1), (-1, 0), (-1, 1), (0, 0), (0, 1))
CIDX = {key: i for i, key in enumerate(CHUNKS)}


def pair_row(col, off):
    return ((off % 8) * 2 + col) * CAP


def dot(a, b):
    return jnp.dot(a, b, preferred_element_type=F32)


def dot_t(a, b):
    return lax.dot_general(a, b, (((1,), (1,)), ((), ())), preferred_element_type=F32)


def routed_rows(ids):
    routed = jnp.logical_or(ids[0:1, :] == 0, ids[1:2, :] == 0)
    n_tok = routed.shape[1]
    routed_f = jnp.where(routed, 1.0, 0.0).astype(F32)
    before = (
        lax.broadcasted_iota(jnp.int32, (n_tok, n_tok), 0)
        < lax.broadcasted_iota(jnp.int32, (n_tok, n_tok), 1)
    )
    rank = dot(
        jnp.broadcast_to(routed_f, (16, n_tok)).astype(BF),
        jnp.where(before, 1.0, 0.0).astype(BF),
    )[0:1, :]
    slot_no = lax.broadcasted_iota(jnp.int32, (CAP, n_tok), 0).astype(F32)
    chosen = jnp.logical_and(
        jnp.broadcast_to(rank, (CAP, n_tok)) == slot_no,
        jnp.broadcast_to(routed_f, (CAP, n_tok)) > 0.5,
    )
    return jnp.where(chosen, 1.0, 0.0).astype(F32)


def kernel(
    ids_h, prob_h, tokens_h, out_grad_h, w_gate_h, w_up_h, w_down_h,
    o_tok, o_prob, o_w,
    ids, prob, tokens, out_grad, wg, wu, wd, wgt, wut, xs, ds, xt, dt, gs, tp, pb, ws, sr, xa, xb, yb, yc,
    rp, rph, pr, ry, pry, fw,
    w_sem, o_sem, s_sem, r_sem,
):
    D = xs.shape[1]
    F = wg.shape[1]
    H = D // 2
    rows_own = fw.shape[1]
    half = rows_own // 2
    dp, etp = lax.axis_index("dp"), lax.axis_index("etp")
    x, yh, core = dp // 4, (dp // 2) % 2, dp % 2
    z, yl = etp // 2, etp % 2

    def dp_of(px, ph, pc):
        return px * 4 + ph * 2 + pc

    def y_at(step):
        y = (yh * 2 + yl + step) % 4
        return dp_of(x, y // 2, core), z * 2 + y % 2

    dev = {
        "z+": (dp, ((z + 1) % 8) * 2 + yl),
        "z-": (dp, ((z + 7) % 8) * 2 + yl),
        "y+": y_at(1),
        "y-": y_at(3),
        "x+": (dp_of((x + 1) % 4, yh, core), etp),
        "x-": (dp_of((x + 3) % 4, yh, core), etp),
        "y2": (dp_of(x, 1 - yh, core), etp),
        "c": (dp_of(x, yh, 1 - core), etp),
    }
    barrier = pltpu.get_barrier_semaphore()
    for name in dev:
        pl.semaphore_signal(barrier, inc=1, device_id=dev[name], device_id_type=MESH)

    loads = []

    def load(src, dst):
        cp = pltpu.make_async_copy(src, dst, w_sem.at[len(loads)])
        cp.start()
        loads.append(cp)

    load(ids_h, ids)
    load(prob_h, prob)
    load(tokens_h, tokens)
    load(out_grad_h, out_grad)

    count = [0]
    sent, free = [], list(range(s_sem.shape[0]))

    def drain(n):
        for cp, k in sent[:n]:
            cp.wait_send()
            free.append(k)
        del sent[:n]

    def send(name, src, dst):
        return send_all([(name, src, dst)], src, dst)

    def send_all(items, src, dst):
        i, k = count[0], free.pop(0)
        count[0] += 1

        def copy(name, a, b):
            return pltpu.make_async_remote_copy(
                src_ref=a, dst_ref=b, send_sem=s_sem.at[k], recv_sem=r_sem.at[i],
                device_id=dev[name], device_id_type=MESH,
            )

        for item in items:
            copy(*item).start()
        whole = copy(items[0][0], src, dst)
        sent.append((whole, k))
        return whole

    with jax.named_scope("pack"):
        loads[0].wait()
        sel = routed_rows(ids)
        sel_b = sel.astype(BF)
        loads[1].wait()
        w_own = jnp.sum(sel * prob[...].astype(F32), axis=1, keepdims=True)
        ds[0:CAP, D:] = jnp.broadcast_to(w_own, (CAP, 128)).astype(BF)
        loads[2].wait()
        xs[0:CAP, :] = dot(sel_b, tokens[...]).astype(BF)
        loads[3].wait()
        ds[0:CAP, 0:D] = dot(sel_b, out_grad[...]).astype(BF)
        load(w_gate_h, wg)
        load(w_up_h, wu)
        load(w_down_h, wd)

    with jax.named_scope("barrier_wait"):
        pl.semaphore_wait(barrier, len(dev))

    arriving = {}

    def gsend(name, key, to, part):
        a, b = pl.ds(SLOT[key] * CAP, CAP), pl.ds(SLOT[to] * CAP, CAP)
        buf = xs if part == "x" else ds
        arriving[to + (part,)] = send(name, buf.at[a, :], buf.at[b, :])

    def ysend(off, part):
        buf = xs if part == "x" else ds
        a, b = SLOT[(0, off)] * CAP, SLOT[(1, off)] * CAP
        arriving[(1, off, part)] = send_all(
            [
                (name, buf.at[pl.ds(a + q * HALF, HALF), :], buf.at[pl.ds(b + q * HALF, HALF), :])
                for q, name in ((0, "y+"), (1, "y-"))
            ],
            buf.at[pl.ds(a, CAP), :],
            buf.at[pl.ds(b, CAP), :],
        )

    def gwait(*keys, parts="xd"):
        for key in keys:
            for part in parts:
                arriving.pop(key + (part,)).wait_recv()

    def relay(dist, part):
        for name, sign in (("z+", 1), ("z-", -1)):
            key = (0, sign * dist)
            gwait(key, parts=part)
            if dist < 3:
                gsend(name, key, (0, sign * (dist + 1)), part)
            elif (name, part) in (("z+", "x"), ("z-", "d")):
                gsend(name, key, (0, 4), part)
            ysend(sign * dist, part)

    def forward(first, n):
        m = n * CAP
        rows = slice(first * CAP, first * CAP + m)
        wcol = ds[rows, D:].astype(F32)[:, 0:1]
        n_f = 2
        fw_ = F // n_f
        psum = jnp.zeros((m, 1), F32)
        for f in range(n_f):
            cols = slice(f * fw_, (f + 1) * fw_)
            gate = dot(xs[rows, :], wg[:, cols])
            up = dot(xs[rows, :], wu[:, cols])
            raw = dot_t(ds[rows, 0:D], wd[cols, :])
            sig = 1.0 / (1.0 + jnp.exp(-gate))
            act = gate * sig
            hid = (act * up).astype(BF).astype(F32)
            gh = wcol * raw
            gs[2, rows, cols] = (wcol * hid).astype(BF)
            gs[0, rows, cols] = (gh * up * sig * (1.0 + gate * (1.0 - sig))).astype(BF)
            gs[1, rows, cols] = (gh * act).astype(BF)
            psum = psum + jnp.sum(hid * raw, axis=1, keepdims=True)
        pbr = jnp.broadcast_to(psum, (m, 128))
        for q in range(n):
            r = pair_row(*ORDER[first + q])
            pb[r : r + CAP, :] = pbr[q * CAP : (q + 1) * CAP, :]

    def token_part(first, n, skip=()):
        rows = slice(first * CAP, (first + n) * CAP)

        def tok_tile(i, carry):
            at = pl.multiple_of(i * 512, 512)
            t = (
                dot(gs[0, rows, :], wgt[:, pl.ds(at, 512)])
                + dot(gs[1, rows, :], wut[:, pl.ds(at, 512)])
            ).astype(BF)
            for q in range(n):
                if ORDER[first + q] in skip:
                    continue
                r = pair_row(*ORDER[first + q])
                tp[r : r + CAP, pl.ds(at, 512)] = t[q * CAP : (q + 1) * CAP, :]
            return carry

        lax.fori_loop(0, D // 512, tok_tile, 0)

    def turn(g, src, dst):
        rows = slice(g * 128, (g + 1) * 128)

        def body(n, carry):
            at = pl.multiple_of(n * 256, 256)
            dst[pl.ds(at, 256), rows] = src[rows, pl.ds(at, 256)].T
            return carry

        lax.fori_loop(0, D // 256, body, 0)

    def add_rows(dst, dst_row, src, n, cols):
        def body(i, carry):
            a = pl.ds(pl.multiple_of(dst_row + i * 16, 16), 16)
            b = pl.ds(pl.multiple_of(i * 16, 16), 16)
            dst[a, cols] = (dst[a, cols].astype(F32) + src[b, :].astype(F32)).astype(BF)
            return carry

        lax.fori_loop(0, n // 16, body, 0)

    chain = {}

    def tok_step(c, k):
        sides = ((0, "z+", -1), (1, "z-", 1))
        rows = [pair_row(c, sign * k) for _, _, sign in sides]
        pairs = [pair_row(0, sign * k) for _, _, sign in sides]
        pair = 2 * CAP
        if k < 4:
            before_t, before_p = chain[c, k + 1]
            before_t.wait_recv()
        if k == 4:
            got = send_all(
                [
                    (name, tp.at[pl.ds(rows[i], CAP), slice(i * H, (i + 1) * H)], rph.at[i, c])
                    for i, name, _ in sides
                ],
                tp.at[pl.ds(rows[0], CAP), :],
                tp.at[pl.ds(rows[0], CAP), :],
            )
        else:
            for i, _, _ in sides:
                if k == 3:
                    add_rows(tp, rows[i], rph.at[i, c], CAP, slice(i * H, (i + 1) * H))
                else:
                    add_rows(tp, rows[i], rp.at[c, 2 - k, i], CAP, slice(0, D))
            got = send_all(
                [(name, tp.at[pl.ds(rows[i], CAP), :], rp.at[c, 3 - k, i]) for i, name, _ in sides],
                rp.at[c, 3 - k],
                rp.at[c, 3 - k],
            )
        gotp = None
        if c == 1:
            if k == 4:
                gotp = send("z+", pb.at[pl.ds(pairs[0], pair), :], pr.at[0, 0])
            else:
                before_p.wait_recv()
                for i in (0, 1) if k < 3 else (0,):
                    both = slice(pairs[i], pairs[i] + pair)
                    pb[both, :] = pb[both, :] + pr[3 - k, i]
                gotp = send_all(
                    [
                        (name, pb.at[pl.ds(pairs[i], pair), :], pr.at[4 - k, i])
                        for i, name, _ in sides
                    ],
                    pr.at[4 - k],
                    pr.at[4 - k],
                )
        chain[c, k] = (got, gotp)

    def tok_arrived(c):
        for cp in chain[c, 1]:
            if cp is not None:
                cp.wait_recv()

    own_rows, other_rows = slice(0, CAP), slice(CAP, 2 * CAP)

    def tok_cross():
        tok_arrived(1)

        def body(i, carry):
            a = pl.ds(pl.multiple_of(CAP + i * 16, 16), 16)
            b = pl.ds(pl.multiple_of(i * 16, 16), 16)
            tp[a, :] = (
                tp[a, :].astype(F32) + rp[1, 2, 0, b, :].astype(F32) + rp[1, 2, 1, b, :].astype(F32)
            ).astype(BF)
            return carry

        lax.fori_loop(0, CAP // 16, body, 0)
        pb[other_rows, :] = pb[other_rows, :] + pr[3, 0, other_rows] + pr[3, 1, other_rows]
        crossing = []
        for src, dst in ((tp, ry), (pb, pry)):
            crossing.append(
                send_all(
                    [
                        (name, src.at[pl.ds(CAP + q * HALF, HALF), :], dst.at[pl.ds(q * HALF, HALF), :])
                        for q, name in ((0, "y-"), (1, "y+"))
                    ],
                    src.at[pl.ds(CAP, CAP), :],
                    dst,
                )
            )
        return crossing

    def tok_final(crossing):
        tok_arrived(0)
        for cp in crossing:
            cp.wait_recv()

        def body(i, carry):
            a = pl.ds(pl.multiple_of(i * 16, 16), 16)
            ry[a, :] = (
                tp[a, :].astype(F32) + rp[0, 2, 0, a, :].astype(F32)
                + rp[0, 2, 1, a, :].astype(F32) + ry[a, :].astype(F32)
            ).astype(BF)
            return carry

        lax.fori_loop(0, CAP // 16, body, 0)
        pry[...] = pb[own_rows, :] + pr[3, 0, own_rows] + pr[3, 1, own_rows] + pry[...]
        out(0, ry, o_tok)
        out(1, pry, o_prob)

    outs = []

    def out(i, src, dst):
        cp = pltpu.make_async_copy(src, dst, o_sem.at[i])
        cp.start()
        outs.append(cp)

    def chunk_dot(key, pc, p):
        dx, h = key
        owner = dp_of((x + dx + 4) % 4, (yh + h) % 2, pc)
        at = pl.multiple_of(owner * rows_own, 64)
        lhs = dt if p == 2 else xt
        return dot(lhs[pl.ds(at, rows_own), :], gs[p])

    from_core = {}
    met = set()

    def sib(p, *keys):
        for key in keys:
            ws[p, CIDX[key]] = chunk_dot(key, 1 - core, p).astype(BF)
        at = pl.ds(CIDX[keys[0]], len(keys))
        cp = send("c", ws.at[p, at], sr.at[p, at])
        for key in keys:
            from_core[key, p] = cp

    def own(p, *keys):
        for key in keys:
            i = CIDX[key]
            v = chunk_dot(key, core, p)
            cp = from_core[key, p]
            if id(cp) not in met:
                met.add(id(cp))
                cp.wait_recv()
            sr[p, i] = (v + sr[p, i].astype(F32)).astype(BF)

    far = {}

    def far_send(h, p):
        i = CIDX[(2, h)]
        far[h, p] = send_all(
            [
                (name, sr.at[p, i, pl.ds(q * half, half), :], xa.at[h, p, pl.ds(q * half, half), :])
                for q, name in ((0, "x+"), (1, "x-"))
            ],
            sr.at[p, i],
            xa.at[h, p],
        )

    near = {}

    def near_send(h, p):
        far[h, p].wait_recv()
        for q, dx in ((0, 1), (1, -1)):
            i = CIDX[(dx, h)]
            r = slice(q * half, (q + 1) * half)
            sr[p, i, r, :] = (sr[p, i, r, :].astype(F32) + xa[h, p, r, :].astype(F32)).astype(BF)
        near[h, p] = send_all(
            [
                (name, sr.at[p, CIDX[(dx, h)]], xb.at[h, p, q])
                for q, name, dx in ((0, "x+", 1), (1, "x-", -1))
            ],
            xb.at[h, p],
            xb.at[h, p],
        )

    def near_wait(h, p):
        near[h, p].wait_recv()

    to_y = {}

    def y_last(p):
        near_wait(1, p)
        i = CIDX[(0, 1)]
        sr[p, i] = (
            sr[p, i].astype(F32) + xb[1, p, 0].astype(F32) + xb[1, p, 1].astype(F32)
        ).astype(BF)
        to_y[p] = send("y2", sr.at[p, i], yb.at[p])

    def y_first(dx):
        to_y[2, dx] = send("y2", sr.at[2, CIDX[(dx, 1)]], yc.at[CIDX[(dx, 0)] // 2])

    def y_add(dx):
        to_y[2, dx].wait_recv()
        i = CIDX[(dx, 0)]
        sr[2, i] = (sr[2, i].astype(F32) + yc[i // 2].astype(F32)).astype(BF)

    def w_final(p):
        near_wait(0, p)
        i = CIDX[(0, 0)]
        total = sr[p, i].astype(F32) + xb[0, p, 0].astype(F32) + xb[0, p, 1].astype(F32)
        if p < 2:
            to_y[p].wait_recv()
            total = total + yb[p].astype(F32)
        fw[p] = (total * (1.0 / 16.0)).astype(BF)
        out(2 + p, fw.at[p], o_w.at[p])

    scope = jax.named_scope

    for part in "xd":
        gsend("z+", (0, 0), (0, 1), part)
        gsend("z-", (0, 0), (0, -1), part)
        ysend(0, part)
    with scope("wait_weights"):
        for cp in loads[4:]:
            cp.wait()
    with scope("turn_weights"):
        def turn_weights(n, carry):
            at = pl.multiple_of(n * 256, 256)
            wgt[:, pl.ds(at, 256)] = wg[pl.ds(at, 256), :].T
            wut[:, pl.ds(at, 256)] = wu[pl.ds(at, 256), :].T
            return carry

        lax.fori_loop(0, D // 256, turn_weights, 0)
    with scope("relay_1x"):
        relay(1, "x")
    with scope("relay_1d"):
        relay(1, "d")
        gwait((1, 0))
    with scope("forward_g0"):
        forward(0, 4)
    with scope("token_g0"):
        token_part(0, 4)
    with scope("relay_2x"):
        relay(2, "x")
    with scope("turn_g0"):
        turn(0, xs, xt)
        turn(0, ds, dt)
    with scope("relay_2d"):
        relay(2, "d")
    with scope("wait_g1"):
        gwait((1, 1), (1, -1))
    with scope("forward_g1"):
        forward(4, 4)
    with scope("token_g1"):
        token_part(4, 4)
    with scope("relay_3x"):
        relay(3, "x")
    with scope("turn_g1"):
        turn(1, xs, xt)
        turn(1, ds, dt)
    with scope("relay_3d"):
        relay(3, "d")
    with scope("wait_g2"):
        gwait((1, 2), (1, -2))
    with scope("forward_g2"):
        forward(8, 4)
    with scope("turn_g2"):
        turn(2, xs, xt)
        turn(2, ds, dt)
    with scope("relay_4"):
        for part in "xd":
            gwait((0, 4), parts=part)
            ysend(4, part)
    n_gather = len(sent)
    with scope("far_block"):
        forward(12, 1)
        token_part(12, 1)
    tok_step(0, 4)
    with scope("wait_g3x"):
        gwait((1, 3), (1, -3), (1, 4), parts="x")
    with scope("turn_x"):
        turn(3, xs, xt)
    with scope("wait_g3d"):
        gwait((1, 3), (1, -3), (1, 4), parts="d")
    with scope("forward_g3"):
        forward(12, 4)
    with scope("drain_gather"):
        drain(n_gather)
    with scope("chunks_a"):
        sib(0, (2, 0), (2, 1))
    with scope("token_g23"):
        token_part(8, 8, skip=((0, 4),))
    tok_step(1, 4)
    with scope("far_p0"):
        own(0, (2, 1))
        far_send(1, 0)
        own(0, (2, 0))
        far_send(0, 0)
    with scope("turn_d"):
        turn(3, ds, dt)
    with scope("chunks_b"):
        sib(2, (2, 1))
        sib(2, (1, 1))
        sib(1, (2, 0), (2, 1))
        sib(2, (-1, 1))
        sib(2, (0, 1))
    with scope("tok_0_3"):
        tok_step(0, 3)
    with scope("y_first"):
        own(2, (2, 1))
        y_first(2)
        own(2, (1, 1))
        y_first(1)
    with scope("far_p1"):
        own(1, (2, 1))
        far_send(1, 1)
        own(1, (2, 0))
        far_send(0, 1)
    with scope("y_first_b"):
        own(2, (-1, 1))
        y_first(-1)
        own(2, (0, 1))
        y_first(0)
    with scope("tok_1_3"):
        tok_step(1, 3)
    with scope("chunks_c"):
        sib(0, (1, 0), (1, 1), (-1, 0), (-1, 1))
        sib(1, (1, 0), (1, 1), (-1, 0), (-1, 1))
        own(0, (1, 1), (-1, 1), (1, 0), (-1, 0))
    with scope("near_p0"):
        near_send(1, 0)
        near_send(0, 0)
    with scope("chunks_d"):
        sib(2, (2, 0))
        sib(2, (1, 0))
        sib(2, (-1, 0))
    with scope("tok_0_2"):
        tok_step(0, 2)
    with scope("y_add_2"):
        own(2, (2, 0))
        y_add(2)
        far_send(0, 2)
    with scope("chunks_e"):
        own(1, (1, 1), (-1, 1), (1, 0), (-1, 0))
    with scope("near_p1"):
        near_send(1, 1)
        near_send(0, 1)
    with scope("chunks_f"):
        sib(0, (0, 0), (0, 1))
        sib(1, (0, 0), (0, 1))
        sib(2, (0, 0))
        own(2, (1, 0), (-1, 0))
    with scope("tok_1_2"):
        tok_step(1, 2)
    with scope("chunks_g"):
        own(0, (0, 1), (0, 0))
        own(1, (0, 1), (0, 0))
        own(2, (0, 0))
    with scope("y_add_near"):
        y_add(1)
        y_add(-1)
    with scope("y_last_0"):
        y_last(0)
    with scope("tok_1_1"):
        tok_step(1, 1)
    with scope("tok_0_1"):
        tok_step(0, 1)
    with scope("near_p2"):
        near_send(0, 2)
    with scope("y_add_0"):
        y_add(0)
    with scope("tok_cross"):
        crossing = tok_cross()
    with scope("y_last_1"):
        y_last(1)
    with scope("w_final_0"):
        w_final(0)
    with scope("tok_final"):
        tok_final(crossing)
    with scope("w_final_2"):
        w_final(2)
    with scope("w_final_1"):
        w_final(1)
    with scope("drain"):
        drain(len(sent))
        for cp in outs:
            cp.wait()


def finish(ids, packed, psum, w_in, o_tok, o_prob, o_gate, o_up, o_down):
    sel = routed_rows(ids)
    o_gate[...] = w_in[0]
    o_up[...] = w_in[1]
    o_down[...] = w_in[2]
    o_tok[...] = dot(sel.T.astype(BF), packed[...]).astype(BF)
    o_prob[...] = jnp.sum(sel * psum[...], axis=0, keepdims=True)


def shards(tokens, out_grad, route_ids, route_prob, w_gate, w_up, w_down):
    n_tok, D = tokens.shape
    F = w_gate.shape[1]
    own = D // lax.axis_size("dp")
    rows = CAP * lax.axis_size("etp")
    vmem = pl.BlockSpec(memory_space=pltpu.VMEM)
    hbm = pl.BlockSpec(memory_space=pl.ANY)
    n_send, n_recv = 45, 74
    scratch = [
        pltpu.VMEM((2, n_tok), jnp.int32),
        pltpu.VMEM((1, n_tok), BF),
        pltpu.VMEM((n_tok, D), BF),
        pltpu.VMEM((n_tok, D), BF),
        pltpu.VMEM((D, F), BF),
        pltpu.VMEM((D, F), BF),
        pltpu.VMEM((F, D), BF),
        pltpu.VMEM((F, D), BF),
        pltpu.VMEM((F, D), BF),
        pltpu.VMEM((rows, D), BF),
        pltpu.VMEM((rows, D + 128), BF),
        pltpu.VMEM((D, rows), BF),
        pltpu.VMEM((D, rows), BF),
        pltpu.VMEM((3, rows, F), BF),
        pltpu.VMEM((rows, D), BF),
        pltpu.VMEM((rows, 128), F32),
        pltpu.VMEM((3, 8, own, F), BF),
        pltpu.VMEM((3, 8, own, F), BF),
        pltpu.VMEM((2, 3, own, F), BF),
        pltpu.VMEM((2, 3, 2, own, F), BF),
        pltpu.VMEM((2, own, F), BF),
        pltpu.VMEM((4, own, F), BF),
        pltpu.VMEM((2, 3, 2, CAP, D), BF),
        pltpu.VMEM((2, 2, CAP, D // 2), BF),
        pltpu.VMEM((4, 2, 2 * CAP, 128), F32),
        pltpu.VMEM((CAP, D), BF),
        pltpu.VMEM((CAP, 128), F32),
        pltpu.VMEM((3, own, F), BF),
        pltpu.SemaphoreType.DMA((7,)),
        pltpu.SemaphoreType.DMA((5,)),
        pltpu.SemaphoreType.DMA((n_send,)),
        pltpu.SemaphoreType.DMA((n_recv,)),
    ]
    ids = route_ids.T
    packed, psum, g_w = pl.pallas_call(
        kernel,
        out_shape=(
            jax.ShapeDtypeStruct((CAP, D), BF),
            jax.ShapeDtypeStruct((CAP, 128), F32),
            jax.ShapeDtypeStruct((3, own, F), BF),
        ),
        in_specs=[hbm] * 7,
        out_specs=(hbm, hbm, hbm),
        scratch_shapes=scratch,
        compiler_params=pltpu.CompilerParams(
            collective_id=0, has_side_effects=True, vmem_limit_bytes=60 * 1024 * 1024
        ),
        cost_estimate=pl.CostEstimate(
            flops=8 * 2 * rows * D * F, bytes_accessed=6 * D * F + 8 * n_tok * D, transcendentals=rows * F
        ),
    )(ids, route_prob.reshape(1, n_tok), tokens, out_grad, w_gate, w_up, w_down)
    g_tok, g_prob, g_gate, g_up, g_down = pl.pallas_call(
        finish,
        out_shape=(
            jax.ShapeDtypeStruct((n_tok, D), BF),
            jax.ShapeDtypeStruct((1, n_tok), F32),
        )
        + (jax.ShapeDtypeStruct((own, F), BF),) * 3,
        in_specs=[vmem] * 4,
        out_specs=(vmem,) * 5,
    )(ids, packed, psum, g_w)
    return g_tok, g_prob.reshape(n_tok), g_gate, g_up, g_down.T


def solution(mesh):
    placed = (
        P(("dp", "etp"), None),
        P(("dp", "etp"), None),
        P(("dp", "etp"), None),
        P(("dp", "etp")),
        P(None, "etp"),
        P(None, "etp"),
        P("etp", None),
    )
    return jax.shard_map(
        shards,
        mesh=mesh,
        in_specs=placed,
        out_specs=(
            P(("dp", "etp"), None),
            P(("dp", "etp")),
            P("dp", "etp"),
            P("dp", "etp"),
            P("etp", "dp"),
        ),
        check_vma=False,
    )
```

```python
import functools

import jax
import jax.numpy as jnp
from jax import lax
from jax.experimental import pallas as pl
from jax.experimental.pallas import tpu as pltpu
from jax.sharding import PartitionSpec as P

MESH = pl.DeviceIdType.MESH
CAP = 32
BF = jnp.bfloat16
F32 = jnp.float32

ORDER = (
    (0, 0), (1, 0), (0, 1), (0, -1),
    (0, 2), (0, -2), (1, 1), (1, -1),
    (0, 3), (0, -3), (1, 2), (1, -2),
    (0, 4), (1, 3), (1, -3), (1, 4),
)
HALF = CAP // 2
SLOT = {key: i for i, key in enumerate(ORDER)}
CHUNKS = ((2, 0), (2, 1), (1, 0), (1, 1), (-1, 0), (-1, 1), (0, 0), (0, 1))
CIDX = {key: i for i, key in enumerate(CHUNKS)}


def pair_row(col, off):
    return ((off % 8) * 2 + col) * CAP


def dot(a, b):
    return jnp.dot(a, b, preferred_element_type=F32)


def dot_t(a, b):
    return lax.dot_general(a, b, (((1,), (1,)), ((), ())), preferred_element_type=F32)


def routed_rows(ids):
    routed = jnp.logical_or(ids[0:1, :] == 0, ids[1:2, :] == 0)
    n_tok = routed.shape[1]
    routed_f = jnp.where(routed, 1.0, 0.0).astype(F32)
    before = (
        lax.broadcasted_iota(jnp.int32, (n_tok, n_tok), 0)
        < lax.broadcasted_iota(jnp.int32, (n_tok, n_tok), 1)
    )
    rank = dot(
        jnp.broadcast_to(routed_f, (16, n_tok)).astype(BF),
        jnp.where(before, 1.0, 0.0).astype(BF),
    )[0:1, :]
    slot_no = lax.broadcasted_iota(jnp.int32, (CAP, n_tok), 0).astype(F32)
    chosen = jnp.logical_and(
        jnp.broadcast_to(rank, (CAP, n_tok)) == slot_no,
        jnp.broadcast_to(routed_f, (CAP, n_tok)) > 0.5,
    )
    return jnp.where(chosen, 1.0, 0.0).astype(F32)


def kernel(
    ids_h, prob_h, tokens_h, out_grad_h, w_gate_h, w_up_h, w_down_h,
    o_tok, o_prob, o_w,
    ids, prob, tokens, out_grad, wg, wu, wd, wgt, wut, xs, ds, xt, dt, gs, tp, pb, ws, wo, sr, xa, xb, yb, yc,
    rp, rph, pr, ry, pry, fw,
    w_sem, o_sem, s_sem, r_sem,
):
    D = xs.shape[1]
    F = wg.shape[1]
    H = D // 2
    rows_own = fw.shape[1]
    half = rows_own // 2
    dp, etp = lax.axis_index("dp"), lax.axis_index("etp")
    x, yh, core = dp // 4, (dp // 2) % 2, dp % 2
    z, yl = etp // 2, etp % 2

    def dp_of(px, ph, pc):
        return px * 4 + ph * 2 + pc

    def y_at(step):
        y = (yh * 2 + yl + step) % 4
        return dp_of(x, y // 2, core), z * 2 + y % 2

    dev = {
        "z+": (dp, ((z + 1) % 8) * 2 + yl),
        "z-": (dp, ((z + 7) % 8) * 2 + yl),
        "y+": y_at(1),
        "y-": y_at(3),
        "x+": (dp_of((x + 1) % 4, yh, core), etp),
        "x-": (dp_of((x + 3) % 4, yh, core), etp),
        "y2": (dp_of(x, 1 - yh, core), etp),
        "c": (dp_of(x, yh, 1 - core), etp),
    }
    barrier = pltpu.get_barrier_semaphore()
    for name in dev:
        pl.semaphore_signal(barrier, inc=1, device_id=dev[name], device_id_type=MESH)

    scope = jax.named_scope
    loads = []

    def load(src, dst):
        cp = pltpu.make_async_copy(src, dst, w_sem.at[len(loads)])
        cp.start()
        loads.append(cp)

    load(ids_h, ids)
    load(prob_h, prob)
    load(tokens_h, tokens)
    load(out_grad_h, out_grad)

    count = [0]
    sent, free = [], list(range(s_sem.shape[0]))

    def drain(n):
        for cp, k in sent[:n]:
            cp.wait_send()
            free.append(k)
        del sent[:n]

    def send(name, src, dst):
        return send_all([(name, src, dst)], src, dst)

    def send_all(items, src, dst):
        i, k = count[0], free.pop(0)
        count[0] += 1

        def copy(name, a, b):
            return pltpu.make_async_remote_copy(
                src_ref=a, dst_ref=b, send_sem=s_sem.at[k], recv_sem=r_sem.at[i],
                device_id=dev[name], device_id_type=MESH,
            )

        for item in items:
            copy(*item).start()
        whole = copy(items[0][0], src, dst)
        sent.append((whole, k))
        return whole

    with jax.named_scope("pack"):
        loads[0].wait()
        sel = routed_rows(ids)
        sel_b = sel.astype(BF)
        loads[1].wait()
        w_own = jnp.sum(sel * prob[...].astype(F32), axis=1, keepdims=True)
        ds[0:CAP, D:] = jnp.broadcast_to(w_own, (CAP, 128)).astype(BF)
        loads[2].wait()
        xs[0:CAP, :] = dot(sel_b, tokens[...]).astype(BF)

    with jax.named_scope("barrier_wait"):
        pl.semaphore_wait(barrier, len(dev))

    arriving = {}

    def gsend(name, key, to, part):
        a, b = pl.ds(SLOT[key] * CAP, CAP), pl.ds(SLOT[to] * CAP, CAP)
        buf = xs if part == "x" else ds
        arriving[to + (part,)] = send(name, buf.at[a, :], buf.at[b, :])

    def ysend(off, part):
        buf = xs if part == "x" else ds
        a, b = SLOT[(0, off)] * CAP, SLOT[(1, off)] * CAP
        arriving[(1, off, part)] = send_all(
            [
                (name, buf.at[pl.ds(a + q * HALF, HALF), :], buf.at[pl.ds(b + q * HALF, HALF), :])
                for q, name in ((0, "y+"), (1, "y-"))
            ],
            buf.at[pl.ds(a, CAP), :],
            buf.at[pl.ds(b, CAP), :],
        )

    def gwait(*keys, parts="xd"):
        for key in keys:
            for part in parts:
                arriving.pop(key + (part,)).wait_recv()

    def relay(dist, part):
        for name, sign in (("z+", 1), ("z-", -1)):
            key = (0, sign * dist)
            gwait(key, parts=part)
            if dist < 3:
                gsend(name, key, (0, sign * (dist + 1)), part)
            elif (name, part) in (("z+", "x"), ("z-", "d")):
                gsend(name, key, (0, 4), part)
            ysend(sign * dist, part)

    def forward(first, n):
        m = n * CAP
        rows = slice(first * CAP, first * CAP + m)
        wcol = ds[rows, D:].astype(F32)[:, 0:1]
        n_f = 2
        fw_ = F // n_f
        psum = jnp.zeros((m, 1), F32)
        for f in range(n_f):
            cols = slice(f * fw_, (f + 1) * fw_)
            gate = dot(xs[rows, :], wg[:, cols])
            up = dot(xs[rows, :], wu[:, cols])
            raw = dot_t(ds[rows, 0:D], wd[cols, :])
            sig = 1.0 / (1.0 + jnp.exp(-gate))
            act = gate * sig
            hid = (act * up).astype(BF).astype(F32)
            gh = wcol * raw
            gs[2, rows, cols] = (wcol * hid).astype(BF)
            gs[0, rows, cols] = (gh * up * sig * (1.0 + gate * (1.0 - sig))).astype(BF)
            gs[1, rows, cols] = (gh * act).astype(BF)
            psum = psum + jnp.sum(hid * raw, axis=1, keepdims=True)
        pbr = jnp.broadcast_to(psum, (m, 128))
        for q in range(n):
            r = pair_row(*ORDER[first + q])
            pb[r : r + CAP, :] = pbr[q * CAP : (q + 1) * CAP, :]

    def token_part(first, n):
        rows = slice(first * CAP, (first + n) * CAP)

        def tok_tile(i, carry):
            at = pl.multiple_of(i * 512, 512)
            t = (
                dot(gs[0, rows, :], wgt[:, pl.ds(at, 512)])
                + dot(gs[1, rows, :], wut[:, pl.ds(at, 512)])
            ).astype(BF)
            for q in range(n):
                r = pair_row(*ORDER[first + q])
                tp[r : r + CAP, pl.ds(at, 512)] = t[q * CAP : (q + 1) * CAP, :]
            return carry

        lax.fori_loop(0, D // 512, tok_tile, 0)

    def turn(g, src, dst):
        rows = slice(g * 128, (g + 1) * 128)

        def body(n, carry):
            at = pl.multiple_of(n * 256, 256)
            dst[pl.ds(at, 256), rows] = src[rows, pl.ds(at, 256)].T
            return carry

        lax.fori_loop(0, D // 256, body, 0)

    def add_rows(dst, dst_row, src, n, cols):
        def body(i, carry):
            a = pl.ds(pl.multiple_of(dst_row + i * 16, 16), 16)
            b = pl.ds(pl.multiple_of(i * 16, 16), 16)
            dst[a, cols] = (dst[a, cols].astype(F32) + src[b, :].astype(F32)).astype(BF)
            return carry

        lax.fori_loop(0, n // 16, body, 0)

    chain = {}

    def tok_step(c, k):
        sides = ((0, "z+", -1), (1, "z-", 1))
        rows = [pair_row(c, sign * k) for _, _, sign in sides]
        pairs = [pair_row(0, sign * k) for _, _, sign in sides]
        pair = 2 * CAP
        if k < 4:
            before_t, before_p = chain[c, k + 1]
            before_t.wait_recv()
        if k == 4:
            got = send_all(
                [
                    (name, tp.at[pl.ds(rows[i], CAP), slice(i * H, (i + 1) * H)], rph.at[i, c])
                    for i, name, _ in sides
                ],
                tp.at[pl.ds(rows[0], CAP), :],
                tp.at[pl.ds(rows[0], CAP), :],
            )
        else:
            for i, _, _ in sides:
                if k == 3:
                    add_rows(tp, rows[i], rph.at[i, c], CAP, slice(i * H, (i + 1) * H))
                else:
                    add_rows(tp, rows[i], rp.at[c, 2 - k, i], CAP, slice(0, D))
            got = send_all(
                [(name, tp.at[pl.ds(rows[i], CAP), :], rp.at[c, 3 - k, i]) for i, name, _ in sides],
                rp.at[c, 3 - k],
                rp.at[c, 3 - k],
            )
        gotp = None
        if c == 1:
            if k == 4:
                gotp = send("z+", pb.at[pl.ds(pairs[0], pair), :], pr.at[0, 0])
            else:
                before_p.wait_recv()
                for i in (0, 1) if k < 3 else (0,):
                    both = slice(pairs[i], pairs[i] + pair)
                    pb[both, :] = pb[both, :] + pr[3 - k, i]
                gotp = send_all(
                    [
                        (name, pb.at[pl.ds(pairs[i], pair), :], pr.at[4 - k, i])
                        for i, name, _ in sides
                    ],
                    pr.at[4 - k],
                    pr.at[4 - k],
                )
        chain[c, k] = (got, gotp)

    def tok_arrived(c):
        for cp in chain[c, 1]:
            if cp is not None:
                cp.wait_recv()

    own_rows, other_rows = slice(0, CAP), slice(CAP, 2 * CAP)

    def tok_cross():
        tok_arrived(1)

        def body(i, carry):
            a = pl.ds(pl.multiple_of(CAP + i * 16, 16), 16)
            b = pl.ds(pl.multiple_of(i * 16, 16), 16)
            tp[a, :] = (
                tp[a, :].astype(F32) + rp[1, 2, 0, b, :].astype(F32) + rp[1, 2, 1, b, :].astype(F32)
            ).astype(BF)
            return carry

        lax.fori_loop(0, CAP // 16, body, 0)
        pb[other_rows, :] = pb[other_rows, :] + pr[3, 0, other_rows] + pr[3, 1, other_rows]
        crossing = []
        for src, dst in ((tp, ry), (pb, pry)):
            crossing.append(
                send_all(
                    [
                        (name, src.at[pl.ds(CAP + q * HALF, HALF), :], dst.at[pl.ds(q * HALF, HALF), :])
                        for q, name in ((0, "y-"), (1, "y+"))
                    ],
                    src.at[pl.ds(CAP, CAP), :],
                    dst,
                )
            )
        return crossing

    def tok_final(crossing):
        tok_arrived(0)
        for cp in crossing:
            cp.wait_recv()

        def body(i, carry):
            a = pl.ds(pl.multiple_of(i * 16, 16), 16)
            ry[a, :] = (
                tp[a, :].astype(F32) + rp[0, 2, 0, a, :].astype(F32)
                + rp[0, 2, 1, a, :].astype(F32) + ry[a, :].astype(F32)
            ).astype(BF)
            return carry

        lax.fori_loop(0, CAP // 16, body, 0)
        pry[...] = pb[own_rows, :] + pr[3, 0, own_rows] + pr[3, 1, own_rows] + pry[...]
        out(0, ry, o_tok)
        out(1, pry, o_prob)

    outs = []

    def out(i, src, dst):
        cp = pltpu.make_async_copy(src, dst, o_sem.at[i])
        cp.start()
        outs.append(cp)

    early = xs.shape[0] // 2

    def chunk_part(key, pc, p, lo, n):
        dx, h = key
        owner = dp_of((x + dx + 4) % 4, (yh + h) % 2, pc)
        at = pl.multiple_of(owner * rows_own, 64)
        lhs = dt if p == 2 else xt
        return dot(lhs[pl.ds(at, rows_own), lo : lo + n], gs[p, lo : lo + n, :])

    def chunk_early(p, keys=CHUNKS):
        for key in keys:
            ws[p, CIDX[key]] = chunk_part(key, 1 - core, p, 0, early).astype(BF)
            wo[p, CIDX[key]] = chunk_part(key, core, p, 0, early).astype(BF)

    def chunk_dot(key, pc, p, first):
        rest = xs.shape[0] - early
        return chunk_part(key, pc, p, early, rest) + first[p, CIDX[key]].astype(F32)

    from_core = {}
    met = set()

    def sib(p, *keys):
        for key in keys:
            ws[p, CIDX[key]] = chunk_dot(key, 1 - core, p, ws).astype(BF)
        at = pl.ds(CIDX[keys[0]], len(keys))
        cp = send("c", ws.at[p, at], sr.at[p, at])
        for key in keys:
            from_core[key, p] = cp

    def own(p, *keys):
        for key in keys:
            i = CIDX[key]
            v = chunk_dot(key, core, p, wo)
            cp = from_core[key, p]
            if id(cp) not in met:
                met.add(id(cp))
                cp.wait_recv()
            sr[p, i] = (v + sr[p, i].astype(F32)).astype(BF)

    far = {}

    def far_send(h, p):
        i = CIDX[(2, h)]
        far[h, p] = send_all(
            [
                (name, sr.at[p, i, pl.ds(q * half, half), :], xa.at[h, p, pl.ds(q * half, half), :])
                for q, name in ((0, "x+"), (1, "x-"))
            ],
            sr.at[p, i],
            xa.at[h, p],
        )

    near = {}

    def near_send(h, p):
        far[h, p].wait_recv()
        for q, dx in ((0, 1), (1, -1)):
            i = CIDX[(dx, h)]
            r = slice(q * half, (q + 1) * half)
            sr[p, i, r, :] = (sr[p, i, r, :].astype(F32) + xa[h, p, r, :].astype(F32)).astype(BF)
        near[h, p] = send_all(
            [
                (name, sr.at[p, CIDX[(dx, h)]], xb.at[h, p, q])
                for q, name, dx in ((0, "x+", 1), (1, "x-", -1))
            ],
            xb.at[h, p],
            xb.at[h, p],
        )

    def near_wait(h, p):
        near[h, p].wait_recv()

    to_y = {}

    def y_last(p):
        near_wait(1, p)
        i = CIDX[(0, 1)]
        sr[p, i] = (
            sr[p, i].astype(F32) + xb[1, p, 0].astype(F32) + xb[1, p, 1].astype(F32)
        ).astype(BF)
        to_y[p] = send("y2", sr.at[p, i], yb.at[p])

    def y_first(dx):
        to_y[2, dx] = send("y2", sr.at[2, CIDX[(dx, 1)]], yc.at[CIDX[(dx, 0)] // 2])

    def y_add(dx):
        to_y[2, dx].wait_recv()
        i = CIDX[(dx, 0)]
        sr[2, i] = (sr[2, i].astype(F32) + yc[i // 2].astype(F32)).astype(BF)

    def w_final(p):
        near_wait(0, p)
        i = CIDX[(0, 0)]
        total = sr[p, i].astype(F32) + xb[0, p, 0].astype(F32) + xb[0, p, 1].astype(F32)
        if p < 2:
            to_y[p].wait_recv()
            total = total + yb[p].astype(F32)
        fw[p] = (total * (1.0 / 16.0)).astype(BF)
        out(2 + p, fw.at[p], o_w.at[p])

    for part in "xd":
        if part == "d":
            with scope("pack_d"):
                loads[3].wait()
                ds[0:CAP, 0:D] = dot(sel_b, out_grad[...]).astype(BF)
        gsend("z+", (0, 0), (0, 1), part)
        gsend("z-", (0, 0), (0, -1), part)
        ysend(0, part)
    load(w_gate_h, wg)
    load(w_up_h, wu)
    load(w_down_h, wd)
    with scope("wait_weights"):
        for cp in loads[4:]:
            cp.wait()
    with scope("turn_weights"):
        def turn_weights(n, carry):
            at = pl.multiple_of(n * 256, 256)
            wgt[:, pl.ds(at, 256)] = wg[pl.ds(at, 256), :].T
            wut[:, pl.ds(at, 256)] = wu[pl.ds(at, 256), :].T
            return carry

        lax.fori_loop(0, D // 256, turn_weights, 0)
    with scope("relay_1x"):
        relay(1, "x")
    with scope("relay_1d"):
        relay(1, "d")
        gwait((1, 0))
    with scope("forward_g0"):
        forward(0, 4)
    with scope("token_g0"):
        token_part(0, 4)
    with scope("relay_2x"):
        relay(2, "x")
    with scope("turn_g0"):
        turn(0, xs, xt)
        turn(0, ds, dt)
    with scope("relay_2d"):
        relay(2, "d")
    with scope("wait_g1"):
        gwait((1, 1), (1, -1))
    with scope("forward_g1"):
        forward(4, 4)
    with scope("token_g1"):
        token_part(4, 4)
    with scope("relay_3x"):
        relay(3, "x")
    with scope("turn_g1"):
        turn(1, xs, xt)
        turn(1, ds, dt)
    with scope("early_0"):
        chunk_early(0)
        chunk_early(2, CHUNKS[:4])
    with scope("relay_3d"):
        relay(3, "d")
    with scope("wait_g2"):
        gwait((1, 2), (1, -2))
    with scope("turn_g2"):
        turn(2, xs, xt)
        turn(2, ds, dt)
    with scope("early_1"):
        chunk_early(1)
        chunk_early(2, CHUNKS[4:])
    with scope("relay_4"):
        for part in "xd":
            gwait((0, 4), parts=part)
            ysend(4, part)
    n_gather = len(sent)
    with scope("forward_g2"):
        forward(8, 5)
    with scope("token_g2"):
        token_part(8, 5)
    tok_step(0, 4)
    with scope("wait_g3x"):
        gwait((1, 3), (1, -3), (1, 4), parts="x")
    with scope("turn_x"):
        turn(3, xs, xt)
    with scope("wait_g3d"):
        gwait((1, 3), (1, -3), (1, 4), parts="d")
    with scope("forward_g3"):
        forward(13, 3)
    with scope("drain_gather"):
        drain(n_gather)
    with scope("chunks_a"):
        sib(0, (2, 0), (2, 1))
    with scope("tok_0_3"):
        tok_step(0, 3)
    with scope("turn_d"):
        turn(3, ds, dt)
    with scope("chunks_b"):
        sib(1, (2, 0), (2, 1))
        sib(2, (2, 1))
        sib(2, (1, 1))
        sib(2, (-1, 1))
        sib(2, (0, 1))
    with scope("far_p0"):
        own(0, (2, 1))
        far_send(1, 0)
        own(0, (2, 0))
        far_send(0, 0)
    with scope("token_g3"):
        token_part(13, 3)
    tok_step(1, 4)
    with scope("y_first_a"):
        own(2, (2, 1))
        y_first(2)
        own(2, (1, 1))
        y_first(1)
    with scope("far_p1"):
        own(1, (2, 1))
        far_send(1, 1)
        own(1, (2, 0))
        far_send(0, 1)
    with scope("y_first_b"):
        own(2, (-1, 1))
        y_first(-1)
        own(2, (0, 1))
        y_first(0)
    with scope("chunks_c"):
        sib(0, (1, 0), (1, 1), (-1, 0), (-1, 1))
    with scope("tok_1_3"):
        tok_step(1, 3)
    with scope("near_p0"):
        own(0, (1, 1), (-1, 1))
        near_send(1, 0)
        own(0, (1, 0), (-1, 0))
        near_send(0, 0)
    with scope("tok_0_2"):
        tok_step(0, 2)
    with scope("chunks_d"):
        sib(1, (1, 0), (1, 1), (-1, 0), (-1, 1))
        sib(2, (2, 0))
        sib(2, (1, 0))
        sib(2, (-1, 0))
        own(1, (1, 1), (-1, 1), (1, 0), (-1, 0))
        own(2, (2, 0))
    with scope("y_add_2"):
        y_add(2)
        far_send(0, 2)
    with scope("near_p1"):
        near_send(1, 1)
        near_send(0, 1)
    with scope("chunks_f"):
        sib(0, (0, 0), (0, 1))
        sib(1, (0, 0), (0, 1))
        sib(2, (0, 0))
        own(2, (1, 0), (-1, 0))
    with scope("tok_1_2"):
        tok_step(1, 2)
    with scope("chunks_g"):
        own(0, (0, 1), (0, 0))
        own(1, (0, 1), (0, 0))
        own(2, (0, 0))
    with scope("y_add_1"):
        y_add(1)
    with scope("y_last_0"):
        y_last(0)
    with scope("y_add_m1"):
        y_add(-1)
    with scope("tok_1_1"):
        tok_step(1, 1)
    with scope("tok_0_1"):
        tok_step(0, 1)
    with scope("near_p2"):
        near_send(0, 2)
    with scope("y_add_0"):
        y_add(0)
    with scope("y_last_1"):
        y_last(1)
    with scope("w_final_0"):
        w_final(0)
    with scope("tok_cross"):
        crossing = tok_cross()
    with scope("tok_final"):
        tok_final(crossing)
    with scope("w_final_1"):
        w_final(1)
    with scope("w_final_2"):
        w_final(2)
    with scope("drain"):
        drain(len(sent))
        for cp in outs:
            cp.wait()


def finish(ids, packed, psum, w_in, o_tok, o_prob, o_gate, o_up, o_down):
    sel = routed_rows(ids)
    o_gate[...] = w_in[0]
    o_up[...] = w_in[1]
    o_down[...] = w_in[2]
    o_tok[...] = dot(sel.T.astype(BF), packed[...]).astype(BF)
    o_prob[...] = jnp.sum(sel * psum[...], axis=0, keepdims=True)


def shards(tokens, out_grad, route_ids, route_prob, w_gate, w_up, w_down):
    n_tok, D = tokens.shape
    F = w_gate.shape[1]
    own = D // lax.axis_size("dp")
    rows = CAP * lax.axis_size("etp")
    vmem = pl.BlockSpec(memory_space=pltpu.VMEM)
    hbm = pl.BlockSpec(memory_space=pl.ANY)
    n_send, n_recv = 45, 74
    scratch = [
        pltpu.VMEM((2, n_tok), jnp.int32),
        pltpu.VMEM((1, n_tok), BF),
        pltpu.VMEM((n_tok, D), BF),
        pltpu.VMEM((n_tok, D), BF),
        pltpu.VMEM((D, F), BF),
        pltpu.VMEM((D, F), BF),
        pltpu.VMEM((F, D), BF),
        pltpu.VMEM((F, D), BF),
        pltpu.VMEM((F, D), BF),
        pltpu.VMEM((rows, D), BF),
        pltpu.VMEM((rows, D + 128), BF),
        pltpu.VMEM((D, rows), BF),
        pltpu.VMEM((D, rows), BF),
        pltpu.VMEM((3, rows, F), BF),
        pltpu.VMEM((rows, D), BF),
        pltpu.VMEM((rows, 128), F32),
        pltpu.VMEM((3, 8, own, F), BF),
        pltpu.VMEM((3, 8, own, F), BF),
        pltpu.VMEM((3, 8, own, F), BF),
        pltpu.VMEM((2, 3, own, F), BF),
        pltpu.VMEM((2, 3, 2, own, F), BF),
        pltpu.VMEM((2, own, F), BF),
        pltpu.VMEM((4, own, F), BF),
        pltpu.VMEM((2, 3, 2, CAP, D), BF),
        pltpu.VMEM((2, 2, CAP, D // 2), BF),
        pltpu.VMEM((4, 2, 2 * CAP, 128), F32),
        pltpu.VMEM((CAP, D), BF),
        pltpu.VMEM((CAP, 128), F32),
        pltpu.VMEM((3, own, F), BF),
        pltpu.SemaphoreType.DMA((7,)),
        pltpu.SemaphoreType.DMA((5,)),
        pltpu.SemaphoreType.DMA((n_send,)),
        pltpu.SemaphoreType.DMA((n_recv,)),
    ]
    ids = route_ids.T
    packed, psum, g_w = pl.pallas_call(
        kernel,
        out_shape=(
            jax.ShapeDtypeStruct((CAP, D), BF),
            jax.ShapeDtypeStruct((CAP, 128), F32),
            jax.ShapeDtypeStruct((3, own, F), BF),
        ),
        in_specs=[hbm] * 7,
        out_specs=(hbm, hbm, hbm),
        scratch_shapes=scratch,
        compiler_params=pltpu.CompilerParams(
            collective_id=0, has_side_effects=True, vmem_limit_bytes=60 * 1024 * 1024
        ),
        cost_estimate=pl.CostEstimate(
            flops=8 * 2 * rows * D * F, bytes_accessed=6 * D * F + 8 * n_tok * D, transcendentals=rows * F
        ),
    )(ids, route_prob.reshape(1, n_tok), tokens, out_grad, w_gate, w_up, w_down)
    g_tok, g_prob, g_gate, g_up, g_down = pl.pallas_call(
        finish,
        out_shape=(
            jax.ShapeDtypeStruct((n_tok, D), BF),
            jax.ShapeDtypeStruct((1, n_tok), F32),
        )
        + (jax.ShapeDtypeStruct((own, F), BF),) * 3,
        in_specs=[vmem] * 4,
        out_specs=(vmem,) * 5,
    )(ids, packed, psum, g_w)
    return g_tok, g_prob.reshape(n_tok), g_gate, g_up, g_down.T


def solution(mesh):
    placed = (
        P(("dp", "etp"), None),
        P(("dp", "etp"), None),
        P(("dp", "etp"), None),
        P(("dp", "etp")),
        P(None, "etp"),
        P(None, "etp"),
        P("etp", None),
    )
    return jax.shard_map(
        shards,
        mesh=mesh,
        in_specs=placed,
        out_specs=(
            P(("dp", "etp"), None),
            P(("dp", "etp")),
            P("dp", "etp"),
            P("dp", "etp"),
            P("etp", "dp"),
        ),
        check_vma=False,
    )
```

```python
import functools

import jax
import jax.numpy as jnp
from jax import lax
from jax.experimental import pallas as pl
from jax.experimental.pallas import tpu as pltpu
from jax.sharding import PartitionSpec as P

MESH = pl.DeviceIdType.MESH
CAP = 32
BF = jnp.bfloat16
F32 = jnp.float32

ORDER = (
    (0, 0), (1, 0), (0, 1), (0, -1),
    (0, 2), (0, -2), (1, 1), (1, -1),
    (0, 3), (0, -3), (1, 2), (1, -2),
    (0, 4), (1, 3), (1, -3), (1, 4),
)
HALF = CAP // 2
SLOT = {key: i for i, key in enumerate(ORDER)}
CHUNKS = ((2, 0), (2, 1), (1, 0), (1, 1), (-1, 0), (-1, 1), (0, 0), (0, 1))
CIDX = {key: i for i, key in enumerate(CHUNKS)}


def pair_row(col, off):
    return ((off % 8) * 2 + col) * CAP


def dot(a, b):
    return jnp.dot(a, b, preferred_element_type=F32)


def dot_t(a, b):
    return lax.dot_general(a, b, (((1,), (1,)), ((), ())), preferred_element_type=F32)


def diagonal():
    shape = (CAP, 128)
    return lax.broadcasted_iota(jnp.int32, shape, 0) == lax.broadcasted_iota(jnp.int32, shape, 1)


def routed_rows(ids):
    routed = jnp.logical_or(ids[0:1, :] == 0, ids[1:2, :] == 0)
    n_tok = routed.shape[1]
    routed_f = jnp.where(routed, 1.0, 0.0).astype(F32)
    before = (
        lax.broadcasted_iota(jnp.int32, (n_tok, n_tok), 0)
        < lax.broadcasted_iota(jnp.int32, (n_tok, n_tok), 1)
    )
    rank = dot(
        jnp.broadcast_to(routed_f, (16, n_tok)).astype(BF),
        jnp.where(before, 1.0, 0.0).astype(BF),
    )[0:1, :]
    slot_no = lax.broadcasted_iota(jnp.int32, (CAP, n_tok), 0).astype(F32)
    chosen = jnp.logical_and(
        jnp.broadcast_to(rank, (CAP, n_tok)) == slot_no,
        jnp.broadcast_to(routed_f, (CAP, n_tok)) > 0.5,
    )
    return jnp.where(chosen, 1.0, 0.0).astype(F32)


def kernel(
    ids_h, prob_h, tokens_h, out_grad_h, w_gate_h, w_up_h, w_down_h,
    o_tok, o_prob, o_w,
    ids, prob, tokens, out_grad, wg, wu, wd, wgt, wut, xs, ds, xt, dt, gs, tp, pb, ws, wo, sr, xa, xb, yb, yc,
    rp, rph, pr, ry, pry, fp, fw,
    w_sem, o_sem, s_sem, r_sem,
):
    D = xs.shape[1]
    F = wg.shape[1]
    H = D // 2
    rows_own = fw.shape[1]
    half = rows_own // 2
    dp, etp = lax.axis_index("dp"), lax.axis_index("etp")
    x, yh, core = dp // 4, (dp // 2) % 2, dp % 2
    z, yl = etp // 2, etp % 2

    def dp_of(px, ph, pc):
        return px * 4 + ph * 2 + pc

    def y_at(step):
        y = (yh * 2 + yl + step) % 4
        return dp_of(x, y // 2, core), z * 2 + y % 2

    dev = {
        "z+": (dp, ((z + 1) % 8) * 2 + yl),
        "z-": (dp, ((z + 7) % 8) * 2 + yl),
        "y+": y_at(1),
        "y-": y_at(3),
        "x+": (dp_of((x + 1) % 4, yh, core), etp),
        "x-": (dp_of((x + 3) % 4, yh, core), etp),
        "y2": (dp_of(x, 1 - yh, core), etp),
        "c": (dp_of(x, yh, 1 - core), etp),
    }
    barrier = pltpu.get_barrier_semaphore()
    for name in dev:
        pl.semaphore_signal(barrier, inc=1, device_id=dev[name], device_id_type=MESH)

    scope = jax.named_scope
    loads = []

    def load(src, dst):
        cp = pltpu.make_async_copy(src, dst, w_sem.at[len(loads)])
        cp.start()
        loads.append(cp)

    load(ids_h, ids)
    load(prob_h, prob)
    load(tokens_h, tokens)
    load(out_grad_h, out_grad)

    count = [0]
    groups = {"x": 0, "d": 1, "core": 2, "weight": 3, "token": 4, "prob": 5}

    def remote(group, i, name, src, dst):
        return pltpu.make_async_remote_copy(
            src_ref=src, dst_ref=dst, send_sem=s_sem.at[groups[group]], recv_sem=r_sem.at[i],
            device_id=dev[name], device_id_type=MESH,
        )

    def send(group, name, src, dst):
        return send_all(group, [(name, src, dst)], src, dst)

    def send_all(group, items, src, dst):
        i = count[0]
        count[0] += 1
        for name, a, b in items:
            remote(group, i, name, a, b).start()
        return remote(group, i, items[0][0], src, dst)

    def drain(group, ref):
        remote(group, 0, "c", ref, ref).wait_send()

    with jax.named_scope("pack"):
        loads[0].wait()
        sel = routed_rows(ids)
        sel_b = sel.astype(BF)
        loads[1].wait()
        w_own = jnp.sum(sel * prob[...].astype(F32), axis=1, keepdims=True)
        ds[0:CAP, D:] = jnp.broadcast_to(w_own, (CAP, 128)).astype(BF)
        loads[2].wait()
        xs[0:CAP, :] = dot(sel_b, tokens[...]).astype(BF)

    with jax.named_scope("barrier_wait"):
        pl.semaphore_wait(barrier, len(dev))

    arriving = {}

    def gsend(name, key, to, part):
        a, b = pl.ds(SLOT[key] * CAP, CAP), pl.ds(SLOT[to] * CAP, CAP)
        buf = xs if part == "x" else ds
        arriving[to + (part,)] = send(part, name, buf.at[a, :], buf.at[b, :])

    def ysend(off, part):
        buf = xs if part == "x" else ds
        a, b = SLOT[(0, off)] * CAP, SLOT[(1, off)] * CAP
        arriving[(1, off, part)] = send_all(
            part,
            [
                (name, buf.at[pl.ds(a + q * HALF, HALF), :], buf.at[pl.ds(b + q * HALF, HALF), :])
                for q, name in ((0, "y+"), (1, "y-"))
            ],
            buf.at[pl.ds(a, CAP), :],
            buf.at[pl.ds(b, CAP), :],
        )

    def gwait(*keys, parts="xd"):
        for key in keys:
            for part in parts:
                arriving.pop(key + (part,)).wait_recv()

    def relay(dist, part):
        for name, sign in (("z+", 1), ("z-", -1)):
            key = (0, sign * dist)
            gwait(key, parts=part)
            if dist < 3:
                gsend(name, key, (0, sign * (dist + 1)), part)
            elif (name, part) in (("z+", "x"), ("z-", "d")):
                gsend(name, key, (0, 4), part)
            ysend(sign * dist, part)

    def forward(first, n):
        m = n * CAP
        rows = slice(first * CAP, first * CAP + m)
        wcol = ds[rows, D:].astype(F32)[:, 0:1]
        n_f = 2
        fw_ = F // n_f
        psum = jnp.zeros((m, 1), F32)
        for f in range(n_f):
            cols = slice(f * fw_, (f + 1) * fw_)
            gate = dot(xs[rows, :], wg[:, cols])
            up = dot(xs[rows, :], wu[:, cols])
            raw = dot_t(ds[rows, 0:D], wd[cols, :])
            sig = 1.0 / (1.0 + jnp.exp(-gate))
            act = gate * sig
            hid = (act * up).astype(BF).astype(F32)
            gh = wcol * raw
            gs[2, rows, cols] = (wcol * hid).astype(BF)
            gs[0, rows, cols] = (gh * up * sig * (1.0 + gate * (1.0 - sig))).astype(BF)
            gs[1, rows, cols] = (gh * act).astype(BF)
            psum = psum + jnp.sum(hid * raw, axis=1, keepdims=True)
        pbr = jnp.broadcast_to(psum, (m, 128))
        for q in range(n):
            c, off = ORDER[first + q]
            row = jnp.sum(
                jnp.where(diagonal(), pbr[q * CAP : (q + 1) * CAP, :], 0.0), axis=0, keepdims=True
            )
            pb[off % 8, c] = jnp.broadcast_to(row, (8, 128))

    def token_part(first, n):
        rows = slice(first * CAP, (first + n) * CAP)

        def tok_tile(i, carry):
            at = pl.multiple_of(i * 512, 512)
            t = (
                dot(gs[0, rows, :], wgt[:, pl.ds(at, 512)])
                + dot(gs[1, rows, :], wut[:, pl.ds(at, 512)])
            ).astype(BF)
            for q in range(n):
                r = pair_row(*ORDER[first + q])
                tp[r : r + CAP, pl.ds(at, 512)] = t[q * CAP : (q + 1) * CAP, :]
            return carry

        lax.fori_loop(0, D // 512, tok_tile, 0)

    def turn(g, src, dst):
        rows = slice(g * 128, (g + 1) * 128)

        def body(n, carry):
            at = pl.multiple_of(n * 256, 256)
            dst[pl.ds(at, 256), rows] = src[rows, pl.ds(at, 256)].T
            return carry

        lax.fori_loop(0, D // 256, body, 0)

    def add_rows(dst, dst_row, src, n, cols):
        def body(i, carry):
            a = pl.ds(pl.multiple_of(dst_row + i * 16, 16), 16)
            b = pl.ds(pl.multiple_of(i * 16, 16), 16)
            dst[a, cols] = (dst[a, cols].astype(F32) + src[b, :].astype(F32)).astype(BF)
            return carry

        lax.fori_loop(0, n // 16, body, 0)

    chain = {}

    def tok_step(c, k):
        sides = ((0, "z+", -1), (1, "z-", 1))
        rows = [pair_row(c, sign * k) for _, _, sign in sides]
        offs = [sign * k % 8 for _, _, sign in sides]
        if k < 4:
            before_t, before_p = chain[c, k + 1]
            before_t.wait_recv()
        if k == 4:
            got = send_all(
                "token",
                [
                    (name, tp.at[pl.ds(rows[i], CAP), slice(i * H, (i + 1) * H)], rph.at[i, c])
                    for i, name, _ in sides
                ],
                tp.at[pl.ds(rows[0], CAP), :],
                tp.at[pl.ds(rows[0], CAP), :],
            )
        else:
            for i, _, _ in sides:
                if k == 3:
                    add_rows(tp, rows[i], rph.at[i, c], CAP, slice(i * H, (i + 1) * H))
                else:
                    add_rows(tp, rows[i], rp.at[c, 2 - k, i], CAP, slice(0, D))
            got = send_all(
                "token",
                [(name, tp.at[pl.ds(rows[i], CAP), :], rp.at[c, 3 - k, i]) for i, name, _ in sides],
                rp.at[c, 3 - k],
                rp.at[c, 3 - k],
            )
        gotp = None
        if c == 1:
            if k == 4:
                gotp = send("prob", "z+", pb.at[4], pr.at[0, 0])
            else:
                before_p.wait_recv()
                for i in (0, 1) if k < 3 else (0,):
                    pb[offs[i]] = pb[offs[i]] + pr[3 - k, i]
                gotp = send_all(
                    "prob",
                    [(name, pb.at[offs[i]], pr.at[4 - k, i]) for i, name, _ in sides],
                    pr.at[4 - k],
                    pr.at[4 - k],
                )
        chain[c, k] = (got, gotp)

    def tok_arrived(c):
        for cp in chain[c, 1]:
            if cp is not None:
                cp.wait_recv()

    def tok_cross():
        tok_arrived(1)

        def body(i, carry):
            a = pl.ds(pl.multiple_of(CAP + i * 16, 16), 16)
            b = pl.ds(pl.multiple_of(i * 16, 16), 16)
            tp[a, :] = (
                tp[a, :].astype(F32) + rp[1, 2, 0, b, :].astype(F32) + rp[1, 2, 1, b, :].astype(F32)
            ).astype(BF)
            return carry

        lax.fori_loop(0, CAP // 16, body, 0)
        pb[0, 1] = pb[0, 1] + pr[3, 0, 1] + pr[3, 1, 1]
        sides = ((0, "y-"), (1, "y+"))
        return (
            send_all(
                "token",
                [
                    (name, tp.at[pl.ds(CAP + q * HALF, HALF), :], ry.at[pl.ds(q * HALF, HALF), :])
                    for q, name in sides
                ],
                tp.at[pl.ds(CAP, CAP), :],
                ry,
            ),
            send_all("prob", [(name, pb.at[0, 1], pry.at[q]) for q, name in sides], pry, pry),
        )

    def tok_final(crossing):
        tok_arrived(0)
        for cp in crossing:
            cp.wait_recv()

        def body(i, carry):
            a = pl.ds(pl.multiple_of(i * 16, 16), 16)
            ry[a, :] = (
                tp[a, :].astype(F32) + rp[0, 2, 0, a, :].astype(F32)
                + rp[0, 2, 1, a, :].astype(F32) + ry[a, :].astype(F32)
            ).astype(BF)
            return carry

        lax.fori_loop(0, CAP // 16, body, 0)
        lane = lax.broadcasted_iota(jnp.int32, (8, 128), 1)
        fp[...] = pb[0, 0] + pr[3, 0, 0] + pr[3, 1, 0] + jnp.where(lane < HALF, pry[0], pry[1])
        out(0, ry, o_tok)
        out(1, fp, o_prob)

    outs = []

    def out(i, src, dst):
        cp = pltpu.make_async_copy(src, dst, o_sem.at[i])
        cp.start()
        outs.append(cp)

    early = xs.shape[0] // 2

    def chunk_part(key, pc, p, lo, n):
        dx, h = key
        owner = dp_of((x + dx + 4) % 4, (yh + h) % 2, pc)
        at = pl.multiple_of(owner * rows_own, 64)
        lhs = dt if p == 2 else xt
        return dot(lhs[pl.ds(at, rows_own), lo : lo + n], gs[p, lo : lo + n, :])

    def chunk_early(p, keys=CHUNKS):
        for key in keys:
            ws[p, CIDX[key]] = chunk_part(key, 1 - core, p, 0, early).astype(BF)
            wo[p, CIDX[key]] = chunk_part(key, core, p, 0, early).astype(BF)

    def chunk_dot(key, pc, p, first):
        rest = xs.shape[0] - early
        return chunk_part(key, pc, p, early, rest) + first[p, CIDX[key]].astype(F32)

    from_core = {}
    met = set()

    def sib(p, *keys):
        for key in keys:
            ws[p, CIDX[key]] = chunk_dot(key, 1 - core, p, ws).astype(BF)
        at = pl.ds(CIDX[keys[0]], len(keys))
        cp = send("core", "c", ws.at[p, at], sr.at[p, at])
        for key in keys:
            from_core[key, p] = cp

    def own(p, *keys):
        for key in keys:
            i = CIDX[key]
            v = chunk_dot(key, core, p, wo)
            cp = from_core[key, p]
            if id(cp) not in met:
                met.add(id(cp))
                cp.wait_recv()
            sr[p, i] = (v + sr[p, i].astype(F32)).astype(BF)

    far = {}

    def far_send(h, p):
        i = CIDX[(2, h)]
        far[h, p] = send_all(
            "weight",
            [
                (name, sr.at[p, i, pl.ds(q * half, half), :], xa.at[h, p, pl.ds(q * half, half), :])
                for q, name in ((0, "x+"), (1, "x-"))
            ],
            sr.at[p, i],
            xa.at[h, p],
        )

    near = {}

    def near_send(h, p):
        far[h, p].wait_recv()
        for q, dx in ((0, 1), (1, -1)):
            i = CIDX[(dx, h)]
            r = slice(q * half, (q + 1) * half)
            sr[p, i, r, :] = (sr[p, i, r, :].astype(F32) + xa[h, p, r, :].astype(F32)).astype(BF)
        near[h, p] = send_all(
            "weight",
            [
                (name, sr.at[p, CIDX[(dx, h)]], xb.at[h, p, q])
                for q, name, dx in ((0, "x+", 1), (1, "x-", -1))
            ],
            xb.at[h, p],
            xb.at[h, p],
        )

    def near_wait(h, p):
        near[h, p].wait_recv()

    to_y = {}

    def y_last(p):
        near_wait(1, p)
        i = CIDX[(0, 1)]
        sr[p, i] = (
            sr[p, i].astype(F32) + xb[1, p, 0].astype(F32) + xb[1, p, 1].astype(F32)
        ).astype(BF)
        to_y[p] = send("weight", "y2", sr.at[p, i], yb.at[p])

    def y_first(dx):
        to_y[2, dx] = send("weight", "y2", sr.at[2, CIDX[(dx, 1)]], yc.at[CIDX[(dx, 0)] // 2])

    def y_add(dx):
        to_y[2, dx].wait_recv()
        i = CIDX[(dx, 0)]
        sr[2, i] = (sr[2, i].astype(F32) + yc[i // 2].astype(F32)).astype(BF)

    def w_final(p):
        near_wait(0, p)
        i = CIDX[(0, 0)]
        total = sr[p, i].astype(F32) + xb[0, p, 0].astype(F32) + xb[0, p, 1].astype(F32)
        if p < 2:
            to_y[p].wait_recv()
            total = total + yb[p].astype(F32)
        fw[p] = (total * (1.0 / 16.0)).astype(BF)
        out(2 + p, fw.at[p], o_w.at[p])

    for part in "xd":
        if part == "d":
            with scope("pack_d"):
                loads[3].wait()
                ds[0:CAP, 0:D] = dot(sel_b, out_grad[...]).astype(BF)
        gsend("z+", (0, 0), (0, 1), part)
        gsend("z-", (0, 0), (0, -1), part)
        ysend(0, part)
    load(w_gate_h, wg)
    load(w_up_h, wu)
    load(w_down_h, wd)
    with scope("wait_weights"):
        for cp in loads[4:]:
            cp.wait()
    with scope("turn_weights"):
        def turn_weights(n, carry):
            at = pl.multiple_of(n * 256, 256)
            wgt[:, pl.ds(at, 256)] = wg[pl.ds(at, 256), :].T
            wut[:, pl.ds(at, 256)] = wu[pl.ds(at, 256), :].T
            return carry

        lax.fori_loop(0, D // 256, turn_weights, 0)
    with scope("relay_1x"):
        relay(1, "x")
    with scope("relay_1d"):
        relay(1, "d")
        gwait((1, 0))
    with scope("forward_g0"):
        forward(0, 4)
    with scope("token_g0"):
        token_part(0, 4)
    with scope("relay_2x"):
        relay(2, "x")
    with scope("turn_g0"):
        turn(0, xs, xt)
        turn(0, ds, dt)
    with scope("relay_2d"):
        relay(2, "d")
    with scope("wait_g1"):
        gwait((1, 1), (1, -1))
    with scope("forward_g1"):
        forward(4, 4)
    with scope("token_g1"):
        token_part(4, 4)
    with scope("relay_3x"):
        relay(3, "x")
    with scope("turn_g1"):
        turn(1, xs, xt)
        turn(1, ds, dt)
    with scope("early_0"):
        chunk_early(0)
        chunk_early(2, CHUNKS[:4])
    with scope("relay_3d"):
        relay(3, "d")
    with scope("wait_g2"):
        gwait((1, 2), (1, -2))
    with scope("turn_g2"):
        turn(2, xs, xt)
        turn(2, ds, dt)
    with scope("early_1"):
        chunk_early(1)
        chunk_early(2, CHUNKS[4:])
    with scope("relay_4"):
        for part in "xd":
            gwait((0, 4), parts=part)
            ysend(4, part)
    with scope("forward_g2"):
        forward(8, 5)
    with scope("token_g2"):
        token_part(8, 5)
    tok_step(0, 4)
    with scope("wait_g3x"):
        gwait((1, 3), (1, -3), (1, 4), parts="x")
    with scope("turn_x"):
        turn(3, xs, xt)
    with scope("wait_g3d"):
        gwait((1, 3), (1, -3), (1, 4), parts="d")
    with scope("forward_g3"):
        forward(13, 3)
    with scope("chunks_a"):
        sib(0, (2, 0), (2, 1))
    with scope("tok_0_3"):
        tok_step(0, 3)
    with scope("turn_d"):
        turn(3, ds, dt)
    with scope("chunks_b"):
        sib(1, (2, 0), (2, 1))
        sib(2, (2, 1))
        sib(2, (1, 1))
    with scope("far_p0"):
        own(0, (2, 1))
        far_send(1, 0)
        own(0, (2, 0))
        far_send(0, 0)
    with scope("y_first_a"):
        own(2, (2, 1))
        y_first(2)
        own(2, (1, 1))
        y_first(1)
    with scope("token_g3"):
        sib(2, (-1, 1))
        sib(2, (0, 1))
        token_part(13, 3)
    tok_step(1, 4)
    with scope("far_p1"):
        own(1, (2, 1))
        far_send(1, 1)
        own(1, (2, 0))
        far_send(0, 1)
    with scope("y_first_b"):
        own(2, (-1, 1))
        y_first(-1)
        own(2, (0, 1))
        y_first(0)
    with scope("chunks_c"):
        sib(0, (1, 0), (1, 1), (-1, 0), (-1, 1))
        sib(1, (1, 0), (1, 1), (-1, 0), (-1, 1))
    with scope("tok_1_3"):
        tok_step(1, 3)
    with scope("near_p0"):
        own(0, (1, 1), (-1, 1))
        near_send(1, 0)
        own(1, (1, 1), (-1, 1))
    with scope("tok_0_2"):
        tok_step(0, 2)
    with scope("chunks_d"):
        sib(2, (2, 0))
        sib(2, (1, 0))
        sib(2, (-1, 0))
        own(0, (1, 0), (-1, 0))
        own(1, (1, 0), (-1, 0))
        own(2, (2, 0))
    with scope("near_p1"):
        near_send(1, 1)
    with scope("y_add_2"):
        y_add(2)
        far_send(0, 2)
    with scope("near_h0"):
        near_send(0, 0)
        near_send(0, 1)
    with scope("chunks_f"):
        sib(0, (0, 0), (0, 1))
        sib(1, (0, 0), (0, 1))
        sib(2, (0, 0))
        own(2, (1, 0), (-1, 0))
    with scope("tok_1_2"):
        tok_step(1, 2)
    with scope("chunks_g"):
        own(0, (0, 1), (0, 0))
        own(1, (0, 1), (0, 0))
        own(2, (0, 0))
    with scope("y_add_1"):
        y_add(1)
    with scope("y_last_0"):
        y_last(0)
    with scope("y_add_m1"):
        y_add(-1)
    with scope("tok_1_1"):
        tok_step(1, 1)
    with scope("tok_0_1"):
        tok_step(0, 1)
    with scope("near_p2"):
        near_send(0, 2)
    with scope("y_add_0"):
        y_add(0)
    with scope("y_last_1"):
        y_last(1)
    with scope("tok_cross"):
        crossing = tok_cross()
    with scope("w_final_0"):
        w_final(0)
    with scope("tok_final"):
        tok_final(crossing)
    with scope("w_final_1"):
        w_final(1)
    with scope("w_final_2"):
        w_final(2)
    with scope("drain"):
        drain("x", xs.at[pl.ds(0, 15 * CAP)])
        drain("d", ds.at[pl.ds(0, 15 * CAP)])
        drain("core", ws)
        drain("weight", sr.at[:, pl.ds(0, 7)])
        drain("token", tp.at[pl.ds(0, 15 * CAP)])
        drain("prob", pb)
        for cp in outs:
            cp.wait()


def finish(ids, packed, psum, w_in, o_tok, o_prob, o_gate, o_up, o_down):
    sel = routed_rows(ids)
    o_gate[...] = w_in[0]
    o_up[...] = w_in[1]
    o_down[...] = w_in[2]
    o_tok[...] = dot(sel.T.astype(BF), packed[...]).astype(BF)
    prob = jnp.sum(
        jnp.where(diagonal(), jnp.broadcast_to(psum[0:1, :], (CAP, 128)), 0.0), axis=1, keepdims=True
    )
    o_prob[...] = jnp.sum(sel * prob, axis=0, keepdims=True)


def shards(tokens, out_grad, route_ids, route_prob, w_gate, w_up, w_down):
    n_tok, D = tokens.shape
    F = w_gate.shape[1]
    own = D // lax.axis_size("dp")
    rows = CAP * lax.axis_size("etp")
    vmem = pl.BlockSpec(memory_space=pltpu.VMEM)
    hbm = pl.BlockSpec(memory_space=pl.ANY)
    n_send, n_recv = 6, 74
    scratch = [
        pltpu.VMEM((2, n_tok), jnp.int32),
        pltpu.VMEM((1, n_tok), BF),
        pltpu.VMEM((n_tok, D), BF),
        pltpu.VMEM((n_tok, D), BF),
        pltpu.VMEM((D, F), BF),
        pltpu.VMEM((D, F), BF),
        pltpu.VMEM((F, D), BF),
        pltpu.VMEM((F, D), BF),
        pltpu.VMEM((F, D), BF),
        pltpu.VMEM((rows, D), BF),
        pltpu.VMEM((rows, D + 128), BF),
        pltpu.VMEM((D, rows), BF),
        pltpu.VMEM((D, rows), BF),
        pltpu.VMEM((3, rows, F), BF),
        pltpu.VMEM((rows, D), BF),
        pltpu.VMEM((8, 2, 8, 128), F32),
        pltpu.VMEM((3, 8, own, F), BF),
        pltpu.VMEM((3, 8, own, F), BF),
        pltpu.VMEM((3, 8, own, F), BF),
        pltpu.VMEM((2, 3, own, F), BF),
        pltpu.VMEM((2, 3, 2, own, F), BF),
        pltpu.VMEM((2, own, F), BF),
        pltpu.VMEM((4, own, F), BF),
        pltpu.VMEM((2, 3, 2, CAP, D), BF),
        pltpu.VMEM((2, 2, CAP, D // 2), BF),
        pltpu.VMEM((4, 2, 2, 8, 128), F32),
        pltpu.VMEM((CAP, D), BF),
        pltpu.VMEM((2, 8, 128), F32),
        pltpu.VMEM((8, 128), F32),
        pltpu.VMEM((3, own, F), BF),
        pltpu.SemaphoreType.DMA((7,)),
        pltpu.SemaphoreType.DMA((5,)),
        pltpu.SemaphoreType.DMA((n_send,)),
        pltpu.SemaphoreType.DMA((n_recv,)),
    ]
    ids = route_ids.T
    packed, psum, g_w = pl.pallas_call(
        kernel,
        out_shape=(
            jax.ShapeDtypeStruct((CAP, D), BF),
            jax.ShapeDtypeStruct((8, 128), F32),
            jax.ShapeDtypeStruct((3, own, F), BF),
        ),
        in_specs=[hbm] * 7,
        out_specs=(hbm, hbm, hbm),
        scratch_shapes=scratch,
        compiler_params=pltpu.CompilerParams(
            collective_id=0, has_side_effects=True, vmem_limit_bytes=60 * 1024 * 1024
        ),
        cost_estimate=pl.CostEstimate(
            flops=8 * 2 * rows * D * F, bytes_accessed=6 * D * F + 8 * n_tok * D, transcendentals=rows * F
        ),
    )(ids, route_prob.reshape(1, n_tok), tokens, out_grad, w_gate, w_up, w_down)
    g_tok, g_prob, g_gate, g_up, g_down = pl.pallas_call(
        finish,
        out_shape=(
            jax.ShapeDtypeStruct((n_tok, D), BF),
            jax.ShapeDtypeStruct((1, n_tok), F32),
        )
        + (jax.ShapeDtypeStruct((own, F), BF),) * 3,
        in_specs=[vmem] * 4,
        out_specs=(vmem,) * 5,
    )(ids, packed, psum, g_w)
    return g_tok, g_prob.reshape(n_tok), g_gate, g_up, g_down.T


def solution(mesh):
    placed = (
        P(("dp", "etp"), None),
        P(("dp", "etp"), None),
        P(("dp", "etp"), None),
        P(("dp", "etp")),
        P(None, "etp"),
        P(None, "etp"),
        P("etp", None),
    )
    return jax.shard_map(
        shards,
        mesh=mesh,
        in_specs=placed,
        out_specs=(
            P(("dp", "etp"), None),
            P(("dp", "etp")),
            P("dp", "etp"),
            P("dp", "etp"),
            P("etp", "dp"),
        ),
        check_vma=False,
    )
```

```python
import functools

import jax
import jax.numpy as jnp
from jax import lax
from jax.experimental import pallas as pl
from jax.experimental.pallas import tpu as pltpu
from jax.sharding import PartitionSpec as P

MESH = pl.DeviceIdType.MESH
CAP = 32
BF = jnp.bfloat16
F32 = jnp.float32

ORDER = (
    (0, 0), (1, 0), (0, 1), (0, -1),
    (0, 2), (0, -2), (1, 1), (1, -1),
    (0, 3), (0, -3), (1, 2), (1, -2),
    (0, 4), (1, 3), (1, -3), (1, 4),
)
HALF = CAP // 2
SLOT = {key: i for i, key in enumerate(ORDER)}
CHUNKS = ((2, 0), (2, 1), (1, 0), (1, 1), (-1, 0), (-1, 1), (0, 0), (0, 1))
CIDX = {key: i for i, key in enumerate(CHUNKS)}


def pair_row(col, off):
    return ((off % 8) * 2 + col) * CAP


def dot(a, b):
    return jnp.dot(a, b, preferred_element_type=F32)


def dot_t(a, b):
    return lax.dot_general(a, b, (((1,), (1,)), ((), ())), preferred_element_type=F32)


def diagonal():
    shape = (CAP, 128)
    return lax.broadcasted_iota(jnp.int32, shape, 0) == lax.broadcasted_iota(jnp.int32, shape, 1)


def routed_rows(ids):
    routed = jnp.logical_or(ids[0:1, :] == 0, ids[1:2, :] == 0)
    n_tok = routed.shape[1]
    routed_f = jnp.where(routed, 1.0, 0.0).astype(F32)
    before = (
        lax.broadcasted_iota(jnp.int32, (n_tok, n_tok), 0)
        < lax.broadcasted_iota(jnp.int32, (n_tok, n_tok), 1)
    )
    rank = dot(
        jnp.broadcast_to(routed_f, (16, n_tok)).astype(BF),
        jnp.where(before, 1.0, 0.0).astype(BF),
    )[0:1, :]
    slot_no = lax.broadcasted_iota(jnp.int32, (CAP, n_tok), 0).astype(F32)
    chosen = jnp.logical_and(
        jnp.broadcast_to(rank, (CAP, n_tok)) == slot_no,
        jnp.broadcast_to(routed_f, (CAP, n_tok)) > 0.5,
    )
    return jnp.where(chosen, 1.0, 0.0).astype(F32)


def kernel(
    ids_h, prob_h, tokens_h, out_grad_h, w_gate_h, w_up_h, w_down_h,
    o_tok, o_prob, o_w,
    ids, prob, tokens, out_grad, wg, wu, wd, wgt, wut, xs, ds, xt, dt, gs, tp, pb, ws, wo, sr, xa, xb, yb, yc,
    rp, rph, pr, ry, pry, fp, fw,
    w_sem, o_sem, s_sem, r_sem,
):
    D = xs.shape[1]
    F = wg.shape[1]
    H = D // 2
    rows_own = fw.shape[1]
    half = rows_own // 2
    dp, etp = lax.axis_index("dp"), lax.axis_index("etp")
    x, yh, core = dp // 4, (dp // 2) % 2, dp % 2
    z, yl = etp // 2, etp % 2

    def dp_of(px, ph, pc):
        return px * 4 + ph * 2 + pc

    def y_at(step):
        y = (yh * 2 + yl + step) % 4
        return dp_of(x, y // 2, core), z * 2 + y % 2

    dev = {
        "z+": (dp, ((z + 1) % 8) * 2 + yl),
        "z-": (dp, ((z + 7) % 8) * 2 + yl),
        "y+": y_at(1),
        "y-": y_at(3),
        "x+": (dp_of((x + 1) % 4, yh, core), etp),
        "x-": (dp_of((x + 3) % 4, yh, core), etp),
        "y2": (dp_of(x, 1 - yh, core), etp),
        "c": (dp_of(x, yh, 1 - core), etp),
    }
    barrier = pltpu.get_barrier_semaphore()
    for name in dev:
        pl.semaphore_signal(barrier, inc=1, device_id=dev[name], device_id_type=MESH)

    scope = jax.named_scope
    loads = []

    def load(src, dst):
        cp = pltpu.make_async_copy(src, dst, w_sem.at[len(loads)])
        cp.start()
        loads.append(cp)

    load(ids_h, ids)
    load(prob_h, prob)
    load(tokens_h, tokens)
    load(out_grad_h, out_grad)

    count = [0]
    groups = {"x": 0, "d": 1, "core": 2, "weight": 3, "token": 4, "prob": 5}

    def remote(group, i, name, src, dst):
        return pltpu.make_async_remote_copy(
            src_ref=src, dst_ref=dst, send_sem=s_sem.at[groups[group]], recv_sem=r_sem.at[i],
            device_id=dev[name], device_id_type=MESH,
        )

    def send(group, name, src, dst):
        return send_all(group, [(name, src, dst)], src, dst)

    def send_all(group, items, src, dst):
        i = count[0]
        count[0] += 1
        for name, a, b in items:
            remote(group, i, name, a, b).start()
        return remote(group, i, items[0][0], src, dst)

    def drain(group, ref):
        remote(group, 0, "c", ref, ref).wait_send()

    with jax.named_scope("pack"):
        loads[0].wait()
        sel = routed_rows(ids)
        sel_b = sel.astype(BF)
        loads[1].wait()
        w_own = jnp.sum(sel * prob[...].astype(F32), axis=1, keepdims=True)
        ds[0:CAP, D:] = jnp.broadcast_to(w_own, (CAP, 128)).astype(BF)
        loads[2].wait()
        xs[0:CAP, :] = dot(sel_b, tokens[...]).astype(BF)

    with jax.named_scope("barrier_wait"):
        pl.semaphore_wait(barrier, len(dev))

    arriving = {}

    def gsend(name, key, to, part):
        a, b = pl.ds(SLOT[key] * CAP, CAP), pl.ds(SLOT[to] * CAP, CAP)
        buf = xs if part == "x" else ds
        arriving[to + (part,)] = send(part, name, buf.at[a, :], buf.at[b, :])

    def ysend(off, part):
        buf = xs if part == "x" else ds
        a, b = SLOT[(0, off)] * CAP, SLOT[(1, off)] * CAP
        arriving[(1, off, part)] = send_all(
            part,
            [
                (name, buf.at[pl.ds(a + q * HALF, HALF), :], buf.at[pl.ds(b + q * HALF, HALF), :])
                for q, name in ((0, "y+"), (1, "y-"))
            ],
            buf.at[pl.ds(a, CAP), :],
            buf.at[pl.ds(b, CAP), :],
        )

    def gwait(*keys, parts="xd"):
        for key in keys:
            for part in parts:
                arriving.pop(key + (part,)).wait_recv()

    def relay(dist, part):
        for name, sign in (("z+", 1), ("z-", -1)):
            key = (0, sign * dist)
            gwait(key, parts=part)
            if dist < 3:
                gsend(name, key, (0, sign * (dist + 1)), part)
            elif (name, part) in (("z+", "x"), ("z-", "d")):
                gsend(name, key, (0, 4), part)
            ysend(sign * dist, part)

    def forward(first, n):
        m = n * CAP
        rows = slice(first * CAP, first * CAP + m)
        wcol = ds[rows, D:].astype(F32)[:, 0:1]
        n_f = 2
        fw_ = F // n_f
        psum = jnp.zeros((m, 1), F32)
        for f in range(n_f):
            cols = slice(f * fw_, (f + 1) * fw_)
            gate = dot(xs[rows, :], wg[:, cols])
            up = dot(xs[rows, :], wu[:, cols])
            raw = dot_t(ds[rows, 0:D], wd[cols, :])
            sig = 1.0 / (1.0 + jnp.exp(-gate))
            act = gate * sig
            hid = (act * up).astype(BF).astype(F32)
            gh = wcol * raw
            gs[2, rows, cols] = (wcol * hid).astype(BF)
            gs[0, rows, cols] = (gh * up * sig * (1.0 + gate * (1.0 - sig))).astype(BF)
            gs[1, rows, cols] = (gh * act).astype(BF)
            psum = psum + jnp.sum(hid * raw, axis=1, keepdims=True)
        pbr = jnp.broadcast_to(psum, (m, 128))
        for q in range(n):
            c, off = ORDER[first + q]
            row = jnp.sum(
                jnp.where(diagonal(), pbr[q * CAP : (q + 1) * CAP, :], 0.0), axis=0, keepdims=True
            )
            pb[off % 8, c] = jnp.broadcast_to(row, (8, 128))

    def token_part(first, n):
        rows = slice(first * CAP, (first + n) * CAP)

        def tok_tile(i, carry):
            at = pl.multiple_of(i * 512, 512)
            t = (
                dot(gs[0, rows, :], wgt[:, pl.ds(at, 512)])
                + dot(gs[1, rows, :], wut[:, pl.ds(at, 512)])
            ).astype(BF)
            for q in range(n):
                r = pair_row(*ORDER[first + q])
                tp[r : r + CAP, pl.ds(at, 512)] = t[q * CAP : (q + 1) * CAP, :]
            return carry

        lax.fori_loop(0, D // 512, tok_tile, 0)

    def turn(g, src, dst):
        rows = slice(g * 128, (g + 1) * 128)

        def body(n, carry):
            at = pl.multiple_of(n * 256, 256)
            dst[pl.ds(at, 256), rows] = src[rows, pl.ds(at, 256)].T
            return carry

        lax.fori_loop(0, D // 256, body, 0)

    def add_rows(dst, dst_row, src, n, cols):
        def body(i, carry):
            a = pl.ds(pl.multiple_of(dst_row + i * 16, 16), 16)
            b = pl.ds(pl.multiple_of(i * 16, 16), 16)
            dst[a, cols] = (dst[a, cols].astype(F32) + src[b, :].astype(F32)).astype(BF)
            return carry

        lax.fori_loop(0, n // 16, body, 0)

    chain = {}

    def tok_step(c, k):
        sides = ((0, "z+", -1), (1, "z-", 1))
        rows = [pair_row(c, sign * k) for _, _, sign in sides]
        offs = [sign * k % 8 for _, _, sign in sides]
        if k < 4:
            before_t, before_p = chain[c, k + 1]
            before_t.wait_recv()
        if k == 4:
            got = send_all(
                "token",
                [
                    (name, tp.at[pl.ds(rows[i], CAP), slice(i * H, (i + 1) * H)], rph.at[i, c])
                    for i, name, _ in sides
                ],
                tp.at[pl.ds(rows[0], CAP), :],
                tp.at[pl.ds(rows[0], CAP), :],
            )
        else:
            for i, _, _ in sides:
                if k == 3:
                    add_rows(tp, rows[i], rph.at[i, c], CAP, slice(i * H, (i + 1) * H))
                else:
                    add_rows(tp, rows[i], rp.at[c, 2 - k, i], CAP, slice(0, D))
            got = send_all(
                "token",
                [(name, tp.at[pl.ds(rows[i], CAP), :], rp.at[c, 3 - k, i]) for i, name, _ in sides],
                rp.at[c, 3 - k],
                rp.at[c, 3 - k],
            )
        gotp = None
        if c == 1:
            if k == 4:
                gotp = send("prob", "z+", pb.at[4], pr.at[0, 0])
            else:
                before_p.wait_recv()
                for i in (0, 1) if k < 3 else (0,):
                    pb[offs[i]] = pb[offs[i]] + pr[3 - k, i]
                gotp = send_all(
                    "prob",
                    [(name, pb.at[offs[i]], pr.at[4 - k, i]) for i, name, _ in sides],
                    pr.at[4 - k],
                    pr.at[4 - k],
                )
        chain[c, k] = (got, gotp)

    def tok_arrived(c):
        for cp in chain[c, 1]:
            if cp is not None:
                cp.wait_recv()

    def tok_cross():
        tok_arrived(1)

        def body(i, carry):
            a = pl.ds(pl.multiple_of(CAP + i * 16, 16), 16)
            b = pl.ds(pl.multiple_of(i * 16, 16), 16)
            tp[a, :] = (
                tp[a, :].astype(F32) + rp[1, 2, 0, b, :].astype(F32) + rp[1, 2, 1, b, :].astype(F32)
            ).astype(BF)
            return carry

        lax.fori_loop(0, CAP // 16, body, 0)
        pb[0, 1] = pb[0, 1] + pr[3, 0, 1] + pr[3, 1, 1]
        sides = ((0, "y-"), (1, "y+"))
        return (
            send_all(
                "token",
                [
                    (name, tp.at[pl.ds(CAP + q * HALF, HALF), :], ry.at[pl.ds(q * HALF, HALF), :])
                    for q, name in sides
                ],
                tp.at[pl.ds(CAP, CAP), :],
                ry,
            ),
            send_all("prob", [(name, pb.at[0, 1], pry.at[q]) for q, name in sides], pry, pry),
        )

    def tok_final(crossing):
        tok_arrived(0)
        for cp in crossing:
            cp.wait_recv()

        def body(i, carry):
            a = pl.ds(pl.multiple_of(i * 16, 16), 16)
            ry[a, :] = (
                tp[a, :].astype(F32) + rp[0, 2, 0, a, :].astype(F32)
                + rp[0, 2, 1, a, :].astype(F32) + ry[a, :].astype(F32)
            ).astype(BF)
            return carry

        lax.fori_loop(0, CAP // 16, body, 0)
        lane = lax.broadcasted_iota(jnp.int32, (8, 128), 1)
        fp[...] = pb[0, 0] + pr[3, 0, 0] + pr[3, 1, 0] + jnp.where(lane < HALF, pry[0], pry[1])
        out(0, ry, o_tok)
        out(1, fp, o_prob)

    outs = []

    def out(i, src, dst):
        cp = pltpu.make_async_copy(src, dst, o_sem.at[i])
        cp.start()
        outs.append(cp)

    early = xs.shape[0] // 2

    def chunk_part(key, pc, p, lo, n):
        dx, h = key
        owner = dp_of((x + dx + 4) % 4, (yh + h) % 2, pc)
        at = pl.multiple_of(owner * rows_own, 64)
        lhs = dt if p == 2 else xt
        return dot(lhs[pl.ds(at, rows_own), lo : lo + n], gs[p, lo : lo + n, :])

    def chunk_early(p, keys=CHUNKS):
        for key in keys:
            ws[p, CIDX[key]] = chunk_part(key, 1 - core, p, 0, early).astype(BF)
            wo[p, CIDX[key]] = chunk_part(key, core, p, 0, early).astype(BF)

    def chunk_dot(key, pc, p, first):
        rest = xs.shape[0] - early
        return chunk_part(key, pc, p, early, rest) + first[p, CIDX[key]].astype(F32)

    from_core = {}
    met = set()

    def sib(p, *keys):
        for key in keys:
            ws[p, CIDX[key]] = chunk_dot(key, 1 - core, p, ws).astype(BF)
        at = pl.ds(CIDX[keys[0]], len(keys))
        cp = send("core", "c", ws.at[p, at], sr.at[p, at])
        for key in keys:
            from_core[key, p] = cp

    def own(p, *keys):
        for key in keys:
            i = CIDX[key]
            v = chunk_dot(key, core, p, wo)
            cp = from_core[key, p]
            if id(cp) not in met:
                met.add(id(cp))
                cp.wait_recv()
            sr[p, i] = (v + sr[p, i].astype(F32)).astype(BF)

    far = {}

    def far_send(h, p):
        i = CIDX[(2, h)]
        far[h, p] = send_all(
            "weight",
            [
                (name, sr.at[p, i, pl.ds(q * half, half), :], xa.at[h, p, pl.ds(q * half, half), :])
                for q, name in ((0, "x+"), (1, "x-"))
            ],
            sr.at[p, i],
            xa.at[h, p],
        )

    near = {}

    def near_send(h, p):
        far[h, p].wait_recv()
        for q, dx in ((0, 1), (1, -1)):
            i = CIDX[(dx, h)]
            r = slice(q * half, (q + 1) * half)
            sr[p, i, r, :] = (sr[p, i, r, :].astype(F32) + xa[h, p, r, :].astype(F32)).astype(BF)
        near[h, p] = send_all(
            "weight",
            [
                (name, sr.at[p, CIDX[(dx, h)]], xb.at[h, p, q])
                for q, name, dx in ((0, "x+", 1), (1, "x-", -1))
            ],
            xb.at[h, p],
            xb.at[h, p],
        )

    def near_wait(h, p):
        near[h, p].wait_recv()

    to_y = {}

    def y_last(p):
        near_wait(1, p)
        i = CIDX[(0, 1)]
        sr[p, i] = (
            sr[p, i].astype(F32) + xb[1, p, 0].astype(F32) + xb[1, p, 1].astype(F32)
        ).astype(BF)
        to_y[p] = send("weight", "y2", sr.at[p, i], yb.at[p])

    def y_first(dx):
        to_y[2, dx] = send("weight", "y2", sr.at[2, CIDX[(dx, 1)]], yc.at[CIDX[(dx, 0)] // 2])

    def y_add(dx):
        to_y[2, dx].wait_recv()
        i = CIDX[(dx, 0)]
        sr[2, i] = (sr[2, i].astype(F32) + yc[i // 2].astype(F32)).astype(BF)

    def w_final(p):
        near_wait(0, p)
        i = CIDX[(0, 0)]
        total = sr[p, i].astype(F32) + xb[0, p, 0].astype(F32) + xb[0, p, 1].astype(F32)
        if p < 2:
            to_y[p].wait_recv()
            total = total + yb[p].astype(F32)
        fw[p] = (total * (1.0 / 16.0)).astype(BF)
        out(2 + p, fw.at[p], o_w.at[p])

    for part in "xd":
        if part == "d":
            with scope("pack_d"):
                loads[3].wait()
                ds[0:CAP, 0:D] = dot(sel_b, out_grad[...]).astype(BF)
        gsend("z+", (0, 0), (0, 1), part)
        gsend("z-", (0, 0), (0, -1), part)
        ysend(0, part)
    load(w_gate_h, wg)
    load(w_up_h, wu)
    load(w_down_h, wd)
    with scope("wait_weights"):
        for cp in loads[4:]:
            cp.wait()
    with scope("turn_weights"):
        def turn_weights(n, carry):
            at = pl.multiple_of(n * 256, 256)
            wgt[:, pl.ds(at, 256)] = wg[pl.ds(at, 256), :].T
            wut[:, pl.ds(at, 256)] = wu[pl.ds(at, 256), :].T
            return carry

        lax.fori_loop(0, D // 256, turn_weights, 0)
    with scope("relay_1x"):
        relay(1, "x")
    with scope("relay_1d"):
        relay(1, "d")
        gwait((1, 0))
    with scope("forward_g0"):
        forward(0, 4)
    with scope("token_g0"):
        token_part(0, 4)
    with scope("relay_2x"):
        relay(2, "x")
    with scope("turn_g0"):
        turn(0, xs, xt)
        turn(0, ds, dt)
    with scope("relay_2d"):
        relay(2, "d")
    with scope("wait_g1"):
        gwait((1, 1), (1, -1))
    with scope("forward_g1"):
        forward(4, 4)
    with scope("token_g1"):
        token_part(4, 4)
    with scope("relay_3x"):
        relay(3, "x")
    with scope("turn_g1"):
        turn(1, xs, xt)
        turn(1, ds, dt)
    with scope("early_0"):
        chunk_early(0)
        chunk_early(2, CHUNKS[:4])
    with scope("relay_3d"):
        relay(3, "d")
    with scope("wait_g2"):
        gwait((1, 2), (1, -2))
    with scope("turn_g2"):
        turn(2, xs, xt)
        turn(2, ds, dt)
    with scope("early_1"):
        chunk_early(1)
        chunk_early(2, CHUNKS[4:])
    with scope("relay_4"):
        for part in "xd":
            gwait((0, 4), parts=part)
            ysend(4, part)
    with scope("forward_g2"):
        forward(8, 5)
    with scope("token_g2"):
        token_part(8, 5)
    tok_step(0, 4)
    with scope("wait_g3x"):
        gwait((1, 3), (1, -3), (1, 4), parts="x")
    with scope("turn_x"):
        turn(3, xs, xt)
    with scope("wait_g3d"):
        gwait((1, 3), (1, -3), (1, 4), parts="d")
    with scope("forward_g3"):
        forward(13, 3)
    with scope("chunks_a"):
        sib(0, (2, 0), (2, 1))
    with scope("tok_0_3"):
        tok_step(0, 3)
    with scope("turn_d"):
        turn(3, ds, dt)
    with scope("chunks_b"):
        sib(1, (2, 0), (2, 1))
        sib(2, (2, 1))
        sib(2, (1, 1))
    with scope("far_p0"):
        own(0, (2, 1))
        far_send(1, 0)
        own(0, (2, 0))
        far_send(0, 0)
    with scope("token_g3"):
        sib(2, (-1, 1))
        sib(2, (0, 1))
        token_part(13, 3)
    tok_step(1, 4)
    with scope("y_first_a"):
        own(2, (2, 1))
        y_first(2)
        own(2, (1, 1))
        y_first(1)
    with scope("far_p1"):
        own(1, (2, 1))
        far_send(1, 1)
        own(1, (2, 0))
        far_send(0, 1)
    with scope("y_first_b"):
        own(2, (-1, 1))
        y_first(-1)
        own(2, (0, 1))
        y_first(0)
    with scope("chunks_c"):
        sib(0, (1, 0), (1, 1), (-1, 0), (-1, 1))
        sib(1, (1, 0), (1, 1), (-1, 0), (-1, 1))
    with scope("tok_1_3"):
        tok_step(1, 3)
    with scope("near_p0"):
        own(0, (1, 1), (-1, 1))
        near_send(1, 0)
        own(1, (1, 1), (-1, 1))
    with scope("tok_0_2"):
        tok_step(0, 2)
    with scope("chunks_d"):
        sib(2, (2, 0))
        sib(2, (1, 0))
        sib(2, (-1, 0))
        own(0, (1, 0), (-1, 0))
        own(1, (1, 0), (-1, 0))
        own(2, (2, 0))
    with scope("near_p1"):
        near_send(1, 1)
    with scope("y_add_2"):
        y_add(2)
        far_send(0, 2)
    with scope("near_h0"):
        near_send(0, 0)
        near_send(0, 1)
    with scope("chunks_f"):
        sib(0, (0, 0), (0, 1))
        sib(1, (0, 0), (0, 1))
        sib(2, (0, 0))
        own(2, (1, 0), (-1, 0))
    with scope("tok_1_2"):
        tok_step(1, 2)
    with scope("chunks_g"):
        own(0, (0, 1), (0, 0))
        own(1, (0, 1), (0, 0))
        own(2, (0, 0))
    with scope("y_add_1"):
        y_add(1)
    with scope("y_last_0"):
        y_last(0)
    with scope("y_add_m1"):
        y_add(-1)
    with scope("tok_1_1"):
        tok_step(1, 1)
    with scope("tok_0_1"):
        tok_step(0, 1)
    with scope("near_p2"):
        near_send(0, 2)
    with scope("y_add_0"):
        y_add(0)
    with scope("y_last_1"):
        y_last(1)
    with scope("tok_cross"):
        crossing = tok_cross()
    with scope("w_final_0"):
        w_final(0)
    with scope("tok_final"):
        tok_final(crossing)
    with scope("w_final_1"):
        w_final(1)
    with scope("w_final_2"):
        w_final(2)
    with scope("drain"):
        drain("x", xs.at[pl.ds(0, 15 * CAP)])
        drain("d", ds.at[pl.ds(0, 15 * CAP)])
        drain("core", ws)
        drain("weight", sr.at[:, pl.ds(0, 7)])
        drain("token", tp.at[pl.ds(0, 15 * CAP)])
        drain("prob", pb)
        for cp in outs:
            cp.wait()


def finish(ids, packed, psum, w_in, o_tok, o_prob, o_gate, o_up, o_down):
    sel = routed_rows(ids)
    o_gate[...] = w_in[0]
    o_up[...] = w_in[1]
    o_down[...] = w_in[2]
    o_tok[...] = dot(sel.T.astype(BF), packed[...]).astype(BF)
    prob = jnp.sum(
        jnp.where(diagonal(), jnp.broadcast_to(psum[0:1, :], (CAP, 128)), 0.0), axis=1, keepdims=True
    )
    o_prob[...] = jnp.sum(sel * prob, axis=0, keepdims=True)


def shards(tokens, out_grad, route_ids, route_prob, w_gate, w_up, w_down):
    n_tok, D = tokens.shape
    F = w_gate.shape[1]
    own = D // lax.axis_size("dp")
    rows = CAP * lax.axis_size("etp")
    vmem = pl.BlockSpec(memory_space=pltpu.VMEM)
    hbm = pl.BlockSpec(memory_space=pl.ANY)
    n_send, n_recv = 6, 74
    scratch = [
        pltpu.VMEM((2, n_tok), jnp.int32),
        pltpu.VMEM((1, n_tok), BF),
        pltpu.VMEM((n_tok, D), BF),
        pltpu.VMEM((n_tok, D), BF),
        pltpu.VMEM((D, F), BF),
        pltpu.VMEM((D, F), BF),
        pltpu.VMEM((F, D), BF),
        pltpu.VMEM((F, D), BF),
        pltpu.VMEM((F, D), BF),
        pltpu.VMEM((rows, D), BF),
        pltpu.VMEM((rows, D + 128), BF),
        pltpu.VMEM((D, rows), BF),
        pltpu.VMEM((D, rows), BF),
        pltpu.VMEM((3, rows, F), BF),
        pltpu.VMEM((rows, D), BF),
        pltpu.VMEM((8, 2, 8, 128), F32),
        pltpu.VMEM((3, 8, own, F), BF),
        pltpu.VMEM((3, 8, own, F), BF),
        pltpu.VMEM((3, 8, own, F), BF),
        pltpu.VMEM((2, 3, own, F), BF),
        pltpu.VMEM((2, 3, 2, own, F), BF),
        pltpu.VMEM((2, own, F), BF),
        pltpu.VMEM((4, own, F), BF),
        pltpu.VMEM((2, 3, 2, CAP, D), BF),
        pltpu.VMEM((2, 2, CAP, D // 2), BF),
        pltpu.VMEM((4, 2, 2, 8, 128), F32),
        pltpu.VMEM((CAP, D), BF),
        pltpu.VMEM((2, 8, 128), F32),
        pltpu.VMEM((8, 128), F32),
        pltpu.VMEM((3, own, F), BF),
        pltpu.SemaphoreType.DMA((7,)),
        pltpu.SemaphoreType.DMA((5,)),
        pltpu.SemaphoreType.DMA((n_send,)),
        pltpu.SemaphoreType.DMA((n_recv,)),
    ]
    ids = route_ids.T
    packed, psum, g_w = pl.pallas_call(
        kernel,
        out_shape=(
            jax.ShapeDtypeStruct((CAP, D), BF),
            jax.ShapeDtypeStruct((8, 128), F32),
            jax.ShapeDtypeStruct((3, own, F), BF),
        ),
        in_specs=[hbm] * 7,
        out_specs=(hbm, hbm, hbm),
        scratch_shapes=scratch,
        compiler_params=pltpu.CompilerParams(
            collective_id=0, has_side_effects=True, vmem_limit_bytes=60 * 1024 * 1024
        ),
        cost_estimate=pl.CostEstimate(
            flops=8 * 2 * rows * D * F, bytes_accessed=6 * D * F + 8 * n_tok * D, transcendentals=rows * F
        ),
    )(ids, route_prob.reshape(1, n_tok), tokens, out_grad, w_gate, w_up, w_down)
    g_tok, g_prob, g_gate, g_up, g_down = pl.pallas_call(
        finish,
        out_shape=(
            jax.ShapeDtypeStruct((n_tok, D), BF),
            jax.ShapeDtypeStruct((1, n_tok), F32),
        )
        + (jax.ShapeDtypeStruct((own, F), BF),) * 3,
        in_specs=[vmem] * 4,
        out_specs=(vmem,) * 5,
    )(ids, packed, psum, g_w)
    return g_tok, g_prob.reshape(n_tok), g_gate, g_up, g_down.T


def solution(mesh):
    placed = (
        P(("dp", "etp"), None),
        P(("dp", "etp"), None),
        P(("dp", "etp"), None),
        P(("dp", "etp")),
        P(None, "etp"),
        P(None, "etp"),
        P("etp", None),
    )
    return jax.shard_map(
        shards,
        mesh=mesh,
        in_specs=placed,
        out_specs=(
            P(("dp", "etp"), None),
            P(("dp", "etp")),
            P("dp", "etp"),
            P("dp", "etp"),
            P("etp", "dp"),
        ),
        check_vma=False,
    )
```

```python
import functools

import jax
import jax.numpy as jnp
from jax import lax
from jax.experimental import pallas as pl
from jax.experimental.pallas import tpu as pltpu
from jax.sharding import PartitionSpec as P

MESH = pl.DeviceIdType.MESH
CAP = 32
BF = jnp.bfloat16
F32 = jnp.float32

ORDER = (
    (0, 0), (1, 0), (0, 1), (0, -1),
    (0, 2), (0, -2), (1, 1), (1, -1),
    (0, 3), (0, -3), (1, 2), (1, -2),
    (0, 4), (1, 3), (1, -3), (1, 4),
)
HALF = CAP // 2
SLOT = {key: i for i, key in enumerate(ORDER)}
CHUNKS = ((2, 0), (2, 1), (1, 0), (1, 1), (-1, 0), (-1, 1), (0, 0), (0, 1))
CIDX = {key: i for i, key in enumerate(CHUNKS)}


def pair_row(col, off):
    return ((off % 8) * 2 + col) * CAP


def dot(a, b):
    return jnp.dot(a, b, preferred_element_type=F32)


def dot_t(a, b):
    return lax.dot_general(a, b, (((1,), (1,)), ((), ())), preferred_element_type=F32)


def diagonal():
    shape = (CAP, 128)
    return lax.broadcasted_iota(jnp.int32, shape, 0) == lax.broadcasted_iota(jnp.int32, shape, 1)


def routed_rows(ids):
    routed = jnp.logical_or(ids[0:1, :] == 0, ids[1:2, :] == 0)
    n_tok = routed.shape[1]
    routed_f = jnp.where(routed, 1.0, 0.0).astype(F32)
    before = (
        lax.broadcasted_iota(jnp.int32, (n_tok, n_tok), 0)
        < lax.broadcasted_iota(jnp.int32, (n_tok, n_tok), 1)
    )
    rank = dot(
        jnp.broadcast_to(routed_f, (16, n_tok)).astype(BF),
        jnp.where(before, 1.0, 0.0).astype(BF),
    )[0:1, :]
    slot_no = lax.broadcasted_iota(jnp.int32, (CAP, n_tok), 0).astype(F32)
    chosen = jnp.logical_and(
        jnp.broadcast_to(rank, (CAP, n_tok)) == slot_no,
        jnp.broadcast_to(routed_f, (CAP, n_tok)) > 0.5,
    )
    return jnp.where(chosen, 1.0, 0.0).astype(F32)


def kernel(
    ids_h, prob_h, tokens_h, out_grad_h, w_gate_h, w_up_h, w_down_h,
    o_tok, o_prob, o_w,
    ids, prob, tokens, out_grad, wg, wu, wd, wgt, wut, xs, ds, xt, dt, gs, tp, pb, ws, wo, sr, xa, xb, yb, yc,
    rp, rph, pr, ry, pry, fp, fw,
    w_sem, o_sem, s_sem, r_sem,
):
    D = xs.shape[1]
    F = wg.shape[1]
    H = D // 2
    rows_own = fw.shape[1]
    half = rows_own // 2
    dp, etp = lax.axis_index("dp"), lax.axis_index("etp")
    x, yh, core = dp // 4, (dp // 2) % 2, dp % 2
    z, yl = etp // 2, etp % 2

    def dp_of(px, ph, pc):
        return px * 4 + ph * 2 + pc

    def y_at(step):
        y = (yh * 2 + yl + step) % 4
        return dp_of(x, y // 2, core), z * 2 + y % 2

    dev = {
        "z+": (dp, ((z + 1) % 8) * 2 + yl),
        "z-": (dp, ((z + 7) % 8) * 2 + yl),
        "y+": y_at(1),
        "y-": y_at(3),
        "x+": (dp_of((x + 1) % 4, yh, core), etp),
        "x-": (dp_of((x + 3) % 4, yh, core), etp),
        "y2": (dp_of(x, 1 - yh, core), etp),
        "c": (dp_of(x, yh, 1 - core), etp),
    }
    barrier = pltpu.get_barrier_semaphore()
    for name in dev:
        pl.semaphore_signal(barrier, inc=1, device_id=dev[name], device_id_type=MESH)

    scope = jax.named_scope
    loads = []

    def load(src, dst):
        cp = pltpu.make_async_copy(src, dst, w_sem.at[len(loads)])
        cp.start()
        loads.append(cp)

    load(ids_h, ids)
    load(prob_h, prob)
    load(tokens_h, tokens)
    load(out_grad_h, out_grad)

    count = [0]
    groups = {"x": 0, "d": 1, "core": 2, "weight": 3, "token": 4, "prob": 5}

    def remote(group, i, name, src, dst):
        return pltpu.make_async_remote_copy(
            src_ref=src, dst_ref=dst, send_sem=s_sem.at[groups[group]], recv_sem=r_sem.at[i],
            device_id=dev[name], device_id_type=MESH,
        )

    def send(group, name, src, dst):
        return send_all(group, [(name, src, dst)], src, dst)

    def send_all(group, items, src, dst):
        i = count[0]
        count[0] += 1
        for name, a, b in items:
            remote(group, i, name, a, b).start()
        return remote(group, i, items[0][0], src, dst)

    def drain(group, ref):
        remote(group, 0, "c", ref, ref).wait_send()

    with jax.named_scope("pack"):
        loads[0].wait()
        sel = routed_rows(ids)
        sel_b = sel.astype(BF)
        loads[1].wait()
        w_own = jnp.sum(sel * prob[...].astype(F32), axis=1, keepdims=True)
        ds[0:CAP, D:] = jnp.broadcast_to(w_own, (CAP, 128)).astype(BF)
        loads[2].wait()
        xs[0:CAP, :] = dot(sel_b, tokens[...]).astype(BF)

    with jax.named_scope("barrier_wait"):
        pl.semaphore_wait(barrier, len(dev))

    arriving = {}

    def gsend(name, key, to, part):
        a, b = pl.ds(SLOT[key] * CAP, CAP), pl.ds(SLOT[to] * CAP, CAP)
        buf = xs if part == "x" else ds
        arriving[to + (part,)] = send(part, name, buf.at[a, :], buf.at[b, :])

    def ysend(off, part):
        buf = xs if part == "x" else ds
        a, b = SLOT[(0, off)] * CAP, SLOT[(1, off)] * CAP
        arriving[(1, off, part)] = send_all(
            part,
            [
                (name, buf.at[pl.ds(a + q * HALF, HALF), :], buf.at[pl.ds(b + q * HALF, HALF), :])
                for q, name in ((0, "y+"), (1, "y-"))
            ],
            buf.at[pl.ds(a, CAP), :],
            buf.at[pl.ds(b, CAP), :],
        )

    def gwait(*keys, parts="xd"):
        for key in keys:
            for part in parts:
                arriving.pop(key + (part,)).wait_recv()

    def relay(dist, part):
        for name, sign in (("z+", 1), ("z-", -1)):
            key = (0, sign * dist)
            gwait(key, parts=part)
            if dist < 3:
                gsend(name, key, (0, sign * (dist + 1)), part)
            elif (name, part) in (("z+", "x"), ("z-", "d")):
                gsend(name, key, (0, 4), part)
            ysend(sign * dist, part)

    def forward(first, n):
        m = n * CAP
        rows = slice(first * CAP, first * CAP + m)
        wcol = ds[rows, D:].astype(F32)[:, 0:1]
        n_f = 2
        fw_ = F // n_f
        psum = jnp.zeros((m, 1), F32)
        for f in range(n_f):
            cols = slice(f * fw_, (f + 1) * fw_)
            gate = dot(xs[rows, :], wg[:, cols])
            up = dot(xs[rows, :], wu[:, cols])
            raw = dot_t(ds[rows, 0:D], wd[cols, :])
            sig = 1.0 / (1.0 + jnp.exp(-gate))
            act = gate * sig
            hid = (act * up).astype(BF).astype(F32)
            gh = wcol * raw
            gs[2, rows, cols] = (wcol * hid).astype(BF)
            gs[0, rows, cols] = (gh * up * sig * (1.0 + gate * (1.0 - sig))).astype(BF)
            gs[1, rows, cols] = (gh * act).astype(BF)
            psum = psum + jnp.sum(hid * raw, axis=1, keepdims=True)
        pbr = jnp.broadcast_to(psum, (m, 128))
        for q in range(n):
            c, off = ORDER[first + q]
            row = jnp.sum(
                jnp.where(diagonal(), pbr[q * CAP : (q + 1) * CAP, :], 0.0), axis=0, keepdims=True
            )
            pb[off % 8, c] = jnp.broadcast_to(row, (8, 128))

    def token_part(first, n):
        rows = slice(first * CAP, (first + n) * CAP)

        def tok_tile(i, carry):
            at = pl.multiple_of(i * 512, 512)
            t = (
                dot(gs[0, rows, :], wgt[:, pl.ds(at, 512)])
                + dot(gs[1, rows, :], wut[:, pl.ds(at, 512)])
            ).astype(BF)
            for q in range(n):
                r = pair_row(*ORDER[first + q])
                tp[r : r + CAP, pl.ds(at, 512)] = t[q * CAP : (q + 1) * CAP, :]
            return carry

        lax.fori_loop(0, D // 512, tok_tile, 0)

    def turn(g, src, dst):
        rows = slice(g * 128, (g + 1) * 128)

        def body(n, carry):
            at = pl.multiple_of(n * 256, 256)
            dst[pl.ds(at, 256), rows] = src[rows, pl.ds(at, 256)].T
            return carry

        lax.fori_loop(0, D // 256, body, 0)

    def add_rows(dst, dst_row, src, n, cols):
        def body(i, carry):
            a = pl.ds(pl.multiple_of(dst_row + i * 16, 16), 16)
            b = pl.ds(pl.multiple_of(i * 16, 16), 16)
            dst[a, cols] = (dst[a, cols].astype(F32) + src[b, :].astype(F32)).astype(BF)
            return carry

        lax.fori_loop(0, n // 16, body, 0)

    chain = {}

    def tok_step(c, k):
        sides = ((0, "z+", -1), (1, "z-", 1))
        rows = [pair_row(c, sign * k) for _, _, sign in sides]
        offs = [sign * k % 8 for _, _, sign in sides]
        if k < 4:
            before_t, before_p = chain[c, k + 1]
            before_t.wait_recv()
        if k == 4:
            got = send_all(
                "token",
                [
                    (name, tp.at[pl.ds(rows[i], CAP), slice(i * H, (i + 1) * H)], rph.at[i, c])
                    for i, name, _ in sides
                ],
                tp.at[pl.ds(rows[0], CAP), :],
                tp.at[pl.ds(rows[0], CAP), :],
            )
        else:
            for i, _, _ in sides:
                if k == 3:
                    add_rows(tp, rows[i], rph.at[i, c], CAP, slice(i * H, (i + 1) * H))
                else:
                    add_rows(tp, rows[i], rp.at[c, 2 - k, i], CAP, slice(0, D))
            got = send_all(
                "token",
                [(name, tp.at[pl.ds(rows[i], CAP), :], rp.at[c, 3 - k, i]) for i, name, _ in sides],
                rp.at[c, 3 - k],
                rp.at[c, 3 - k],
            )
        gotp = None
        if c == 1:
            if k == 4:
                gotp = send("prob", "z+", pb.at[4], pr.at[0, 0])
            else:
                before_p.wait_recv()
                for i in (0, 1) if k < 3 else (0,):
                    pb[offs[i]] = pb[offs[i]] + pr[3 - k, i]
                gotp = send_all(
                    "prob",
                    [(name, pb.at[offs[i]], pr.at[4 - k, i]) for i, name, _ in sides],
                    pr.at[4 - k],
                    pr.at[4 - k],
                )
        chain[c, k] = (got, gotp)

    def tok_arrived(c):
        for cp in chain[c, 1]:
            if cp is not None:
                cp.wait_recv()

    def tok_cross():
        tok_arrived(1)

        def body(i, carry):
            a = pl.ds(pl.multiple_of(CAP + i * 16, 16), 16)
            b = pl.ds(pl.multiple_of(i * 16, 16), 16)
            tp[a, :] = (
                tp[a, :].astype(F32) + rp[1, 2, 0, b, :].astype(F32) + rp[1, 2, 1, b, :].astype(F32)
            ).astype(BF)
            return carry

        lax.fori_loop(0, CAP // 16, body, 0)
        pb[0, 1] = pb[0, 1] + pr[3, 0, 1] + pr[3, 1, 1]
        sides = ((0, "y-"), (1, "y+"))
        return (
            send_all(
                "token",
                [
                    (name, tp.at[pl.ds(CAP + q * HALF, HALF), :], ry.at[pl.ds(q * HALF, HALF), :])
                    for q, name in sides
                ],
                tp.at[pl.ds(CAP, CAP), :],
                ry,
            ),
            send_all("prob", [(name, pb.at[0, 1], pry.at[q]) for q, name in sides], pry, pry),
        )

    def tok_final(crossing):
        tok_arrived(0)
        for cp in crossing:
            cp.wait_recv()

        def body(i, carry):
            a = pl.ds(pl.multiple_of(i * 16, 16), 16)
            ry[a, :] = (
                tp[a, :].astype(F32) + rp[0, 2, 0, a, :].astype(F32)
                + rp[0, 2, 1, a, :].astype(F32) + ry[a, :].astype(F32)
            ).astype(BF)
            return carry

        lax.fori_loop(0, CAP // 16, body, 0)
        lane = lax.broadcasted_iota(jnp.int32, (8, 128), 1)
        fp[...] = pb[0, 0] + pr[3, 0, 0] + pr[3, 1, 0] + jnp.where(lane < HALF, pry[0], pry[1])
        out(0, ry, o_tok)
        out(1, fp, o_prob)

    outs = []

    def out(i, src, dst):
        cp = pltpu.make_async_copy(src, dst, o_sem.at[i])
        cp.start()
        outs.append(cp)

    early = xs.shape[0] // 2

    def chunk_part(key, pc, p, lo, n):
        dx, h = key
        owner = dp_of((x + dx + 4) % 4, (yh + h) % 2, pc)
        at = pl.multiple_of(owner * rows_own, 64)
        lhs = dt if p == 2 else xt
        return dot(lhs[pl.ds(at, rows_own), lo : lo + n], gs[p, lo : lo + n, :])

    def chunk_early(p, keys=CHUNKS):
        for key in keys:
            ws[p, CIDX[key]] = chunk_part(key, 1 - core, p, 0, early).astype(BF)
            wo[p, CIDX[key]] = chunk_part(key, core, p, 0, early).astype(BF)

    def chunk_dot(key, pc, p, first):
        rest = xs.shape[0] - early
        return chunk_part(key, pc, p, early, rest) + first[p, CIDX[key]].astype(F32)

    from_core = {}
    met = set()

    def sib(p, *keys):
        for key in keys:
            ws[p, CIDX[key]] = chunk_dot(key, 1 - core, p, ws).astype(BF)
        at = pl.ds(CIDX[keys[0]], len(keys))
        cp = send("core", "c", ws.at[p, at], sr.at[p, at])
        for key in keys:
            from_core[key, p] = cp

    def own(p, *keys):
        for key in keys:
            i = CIDX[key]
            v = chunk_dot(key, core, p, wo)
            cp = from_core[key, p]
            if id(cp) not in met:
                met.add(id(cp))
                cp.wait_recv()
            sr[p, i] = (v + sr[p, i].astype(F32)).astype(BF)

    far = {}

    def far_send(h, p):
        i = CIDX[(2, h)]
        far[h, p] = send_all(
            "weight",
            [
                (name, sr.at[p, i, pl.ds(q * half, half), :], xa.at[h, p, pl.ds(q * half, half), :])
                for q, name in ((0, "x+"), (1, "x-"))
            ],
            sr.at[p, i],
            xa.at[h, p],
        )

    near = {}

    def near_send(h, p):
        far[h, p].wait_recv()
        for q, dx in ((0, 1), (1, -1)):
            i = CIDX[(dx, h)]
            r = slice(q * half, (q + 1) * half)
            sr[p, i, r, :] = (sr[p, i, r, :].astype(F32) + xa[h, p, r, :].astype(F32)).astype(BF)
        near[h, p] = send_all(
            "weight",
            [
                (name, sr.at[p, CIDX[(dx, h)]], xb.at[h, p, q])
                for q, name, dx in ((0, "x+", 1), (1, "x-", -1))
            ],
            xb.at[h, p],
            xb.at[h, p],
        )

    def near_wait(h, p):
        near[h, p].wait_recv()

    to_y = {}

    def y_last(p):
        near_wait(1, p)
        i = CIDX[(0, 1)]
        sr[p, i] = (
            sr[p, i].astype(F32) + xb[1, p, 0].astype(F32) + xb[1, p, 1].astype(F32)
        ).astype(BF)
        to_y[p] = send("weight", "y2", sr.at[p, i], yb.at[p])

    def y_first(dx):
        to_y[2, dx] = send("weight", "y2", sr.at[2, CIDX[(dx, 1)]], yc.at[CIDX[(dx, 0)] // 2])

    def y_add(dx):
        to_y[2, dx].wait_recv()
        i = CIDX[(dx, 0)]
        sr[2, i] = (sr[2, i].astype(F32) + yc[i // 2].astype(F32)).astype(BF)

    def w_final(p):
        near_wait(0, p)
        i = CIDX[(0, 0)]
        total = sr[p, i].astype(F32) + xb[0, p, 0].astype(F32) + xb[0, p, 1].astype(F32)
        if p < 2:
            to_y[p].wait_recv()
            total = total + yb[p].astype(F32)
        fw[p] = (total * (1.0 / 16.0)).astype(BF)
        out(2 + p, fw.at[p], o_w.at[p])

    for part in "xd":
        if part == "d":
            with scope("pack_d"):
                loads[3].wait()
                ds[0:CAP, 0:D] = dot(sel_b, out_grad[...]).astype(BF)
        gsend("z+", (0, 0), (0, 1), part)
        gsend("z-", (0, 0), (0, -1), part)
        ysend(0, part)
    load(w_gate_h, wg)
    load(w_up_h, wu)
    load(w_down_h, wd)
    with scope("wait_weights"):
        for cp in loads[4:]:
            cp.wait()
    with scope("turn_weights"):
        def turn_weights(n, carry):
            at = pl.multiple_of(n * 256, 256)
            wgt[:, pl.ds(at, 256)] = wg[pl.ds(at, 256), :].T
            wut[:, pl.ds(at, 256)] = wu[pl.ds(at, 256), :].T
            return carry

        lax.fori_loop(0, D // 256, turn_weights, 0)
    with scope("relay_1x"):
        relay(1, "x")
    with scope("relay_1d"):
        relay(1, "d")
        gwait((1, 0))
    with scope("forward_g0"):
        forward(0, 4)
    with scope("token_g0"):
        token_part(0, 4)
    with scope("relay_2x"):
        relay(2, "x")
    with scope("turn_g0"):
        turn(0, xs, xt)
        turn(0, ds, dt)
    with scope("relay_2d"):
        relay(2, "d")
    with scope("wait_g1"):
        gwait((1, 1), (1, -1))
    with scope("forward_g1"):
        forward(4, 4)
    with scope("token_g1"):
        token_part(4, 4)
    with scope("relay_3x"):
        relay(3, "x")
    with scope("turn_g1"):
        turn(1, xs, xt)
        turn(1, ds, dt)
    with scope("early_0"):
        chunk_early(0)
        chunk_early(2, CHUNKS[:4])
    with scope("relay_3d"):
        relay(3, "d")
    with scope("wait_g2"):
        gwait((1, 2), (1, -2))
    with scope("turn_g2"):
        turn(2, xs, xt)
        turn(2, ds, dt)
    with scope("early_1"):
        chunk_early(1)
        chunk_early(2, CHUNKS[4:])
    with scope("relay_4"):
        for part in "xd":
            gwait((0, 4), parts=part)
            ysend(4, part)
    with scope("forward_g2"):
        forward(8, 5)
    with scope("token_g2"):
        token_part(8, 5)
    tok_step(0, 4)
    with scope("wait_g3x"):
        gwait((1, 3), (1, -3), (1, 4), parts="x")
    with scope("turn_x"):
        turn(3, xs, xt)
    with scope("wait_g3d"):
        gwait((1, 3), (1, -3), (1, 4), parts="d")
    with scope("forward_g3"):
        forward(13, 3)
    with scope("chunks_a"):
        sib(0, (2, 1))
        sib(0, (2, 0))
    with scope("tok_0_3"):
        tok_step(0, 3)
    with scope("turn_d"):
        turn(3, ds, dt)
    with scope("chunks_b"):
        sib(1, (2, 0), (2, 1))
    with scope("far_p0"):
        own(0, (2, 1))
        far_send(1, 0)
        own(0, (2, 0))
        far_send(0, 0)
    with scope("token_g3"):
        sib(2, (2, 1))
        sib(2, (1, 1))
        sib(2, (-1, 1))
        sib(2, (0, 1))
        token_part(13, 3)
    tok_step(1, 4)
    with scope("y_first_a"):
        own(2, (2, 1))
        y_first(2)
        own(2, (1, 1))
        y_first(1)
    with scope("far_p1"):
        own(1, (2, 1))
        far_send(1, 1)
        own(1, (2, 0))
        far_send(0, 1)
    with scope("y_first_b"):
        own(2, (-1, 1))
        y_first(-1)
        own(2, (0, 1))
        y_first(0)
    with scope("chunks_c"):
        sib(0, (1, 0), (1, 1), (-1, 0), (-1, 1))
        sib(1, (1, 0), (1, 1), (-1, 0), (-1, 1))
    with scope("tok_1_3"):
        tok_step(1, 3)
    with scope("near_p0"):
        own(0, (1, 1), (-1, 1))
        near_send(1, 0)
        own(1, (1, 1), (-1, 1))
    with scope("tok_0_2"):
        tok_step(0, 2)
    with scope("chunks_d"):
        sib(2, (2, 0))
        sib(2, (1, 0))
        sib(2, (-1, 0))
        own(0, (1, 0), (-1, 0))
        own(1, (1, 0), (-1, 0))
        own(2, (2, 0))
    with scope("near_p1"):
        near_send(1, 1)
    with scope("y_add_2"):
        y_add(2)
        far_send(0, 2)
    with scope("near_h0"):
        near_send(0, 0)
        near_send(0, 1)
    with scope("chunks_f"):
        sib(0, (0, 0), (0, 1))
        sib(1, (0, 0), (0, 1))
        sib(2, (0, 0))
        own(2, (1, 0), (-1, 0))
    with scope("tok_1_2"):
        tok_step(1, 2)
    with scope("chunks_g"):
        own(0, (0, 1), (0, 0))
        own(1, (0, 1), (0, 0))
        own(2, (0, 0))
    with scope("y_add_1"):
        y_add(1)
    with scope("y_last_0"):
        y_last(0)
    with scope("y_add_m1"):
        y_add(-1)
    with scope("tok_1_1"):
        tok_step(1, 1)
    with scope("tok_0_1"):
        tok_step(0, 1)
    with scope("near_p2"):
        near_send(0, 2)
    with scope("y_add_0"):
        y_add(0)
    with scope("y_last_1"):
        y_last(1)
    with scope("tok_cross"):
        crossing = tok_cross()
    with scope("w_final_0"):
        w_final(0)
    with scope("tok_final"):
        tok_final(crossing)
    with scope("w_final_1"):
        w_final(1)
    with scope("w_final_2"):
        w_final(2)
    with scope("drain"):
        drain("x", xs.at[pl.ds(0, 15 * CAP)])
        drain("d", ds.at[pl.ds(0, 15 * CAP)])
        drain("core", ws)
        drain("weight", sr.at[:, pl.ds(0, 7)])
        drain("token", tp.at[pl.ds(0, 15 * CAP)])
        drain("prob", pb)
        for cp in outs:
            cp.wait()


def finish(ids, packed, psum, w_in, o_tok, o_prob, o_gate, o_up, o_down):
    sel = routed_rows(ids)
    o_gate[...] = w_in[0]
    o_up[...] = w_in[1]
    o_down[...] = w_in[2]
    o_tok[...] = dot(sel.T.astype(BF), packed[...]).astype(BF)
    prob = jnp.sum(
        jnp.where(diagonal(), jnp.broadcast_to(psum[0:1, :], (CAP, 128)), 0.0), axis=1, keepdims=True
    )
    o_prob[...] = jnp.sum(sel * prob, axis=0, keepdims=True)


def shards(tokens, out_grad, route_ids, route_prob, w_gate, w_up, w_down):
    n_tok, D = tokens.shape
    F = w_gate.shape[1]
    own = D // lax.axis_size("dp")
    rows = CAP * lax.axis_size("etp")
    vmem = pl.BlockSpec(memory_space=pltpu.VMEM)
    hbm = pl.BlockSpec(memory_space=pl.ANY)
    n_send, n_recv = 6, 75
    scratch = [
        pltpu.VMEM((2, n_tok), jnp.int32),
        pltpu.VMEM((1, n_tok), BF),
        pltpu.VMEM((n_tok, D), BF),
        pltpu.VMEM((n_tok, D), BF),
        pltpu.VMEM((D, F), BF),
        pltpu.VMEM((D, F), BF),
        pltpu.VMEM((F, D), BF),
        pltpu.VMEM((F, D), BF),
        pltpu.VMEM((F, D), BF),
        pltpu.VMEM((rows, D), BF),
        pltpu.VMEM((rows, D + 128), BF),
        pltpu.VMEM((D, rows), BF),
        pltpu.VMEM((D, rows), BF),
        pltpu.VMEM((3, rows, F), BF),
        pltpu.VMEM((rows, D), BF),
        pltpu.VMEM((8, 2, 8, 128), F32),
        pltpu.VMEM((3, 8, own, F), BF),
        pltpu.VMEM((3, 8, own, F), BF),
        pltpu.VMEM((3, 8, own, F), BF),
        pltpu.VMEM((2, 3, own, F), BF),
        pltpu.VMEM((2, 3, 2, own, F), BF),
        pltpu.VMEM((2, own, F), BF),
        pltpu.VMEM((4, own, F), BF),
        pltpu.VMEM((2, 3, 2, CAP, D), BF),
        pltpu.VMEM((2, 2, CAP, D // 2), BF),
        pltpu.VMEM((4, 2, 2, 8, 128), F32),
        pltpu.VMEM((CAP, D), BF),
        pltpu.VMEM((2, 8, 128), F32),
        pltpu.VMEM((8, 128), F32),
        pltpu.VMEM((3, own, F), BF),
        pltpu.SemaphoreType.DMA((7,)),
        pltpu.SemaphoreType.DMA((5,)),
        pltpu.SemaphoreType.DMA((n_send,)),
        pltpu.SemaphoreType.DMA((n_recv,)),
    ]
    ids = route_ids.T
    packed, psum, g_w = pl.pallas_call(
        kernel,
        out_shape=(
            jax.ShapeDtypeStruct((CAP, D), BF),
            jax.ShapeDtypeStruct((8, 128), F32),
            jax.ShapeDtypeStruct((3, own, F), BF),
        ),
        in_specs=[hbm] * 7,
        out_specs=(hbm, hbm, hbm),
        scratch_shapes=scratch,
        compiler_params=pltpu.CompilerParams(
            collective_id=0, has_side_effects=True, vmem_limit_bytes=60 * 1024 * 1024
        ),
        cost_estimate=pl.CostEstimate(
            flops=8 * 2 * rows * D * F, bytes_accessed=6 * D * F + 8 * n_tok * D, transcendentals=rows * F
        ),
    )(ids, route_prob.reshape(1, n_tok), tokens, out_grad, w_gate, w_up, w_down)
    g_tok, g_prob, g_gate, g_up, g_down = pl.pallas_call(
        finish,
        out_shape=(
            jax.ShapeDtypeStruct((n_tok, D), BF),
            jax.ShapeDtypeStruct((1, n_tok), F32),
        )
        + (jax.ShapeDtypeStruct((own, F), BF),) * 3,
        in_specs=[vmem] * 4,
        out_specs=(vmem,) * 5,
    )(ids, packed, psum, g_w)
    return g_tok, g_prob.reshape(n_tok), g_gate, g_up, g_down.T


def solution(mesh):
    placed = (
        P(("dp", "etp"), None),
        P(("dp", "etp"), None),
        P(("dp", "etp"), None),
        P(("dp", "etp")),
        P(None, "etp"),
        P(None, "etp"),
        P("etp", None),
    )
    return jax.shard_map(
        shards,
        mesh=mesh,
        in_specs=placed,
        out_specs=(
            P(("dp", "etp"), None),
            P(("dp", "etp")),
            P("dp", "etp"),
            P("dp", "etp"),
            P("etp", "dp"),
        ),
        check_vma=False,
    )
```
